256 devices in a mesh: blk: 32 (over z, y_lo, core), group: 8 (over x, y_hi).
Axes of the slice: x: 4, y: 4 (y_hi: 2, y_lo: 2; y = y_hi * 2 + y_lo), z: 8, core: 2. Of those that a mesh axis runs over, the one named last changes fastest.
Arguments:
- image_embed: bfloat16 [32768, 1152], P(('group', 'blk')), parts along dimension 0, may hold values from -0.5 to 0.5
- text_embed: bfloat16 [32768, 1152], P(('group', 'blk')), parts along dimension 0, may hold values from -0.5 to 0.5
- logit_scale: float32 [1], replicated, may hold values from 4 to 12
- logit_bias: float32 [1], replicated, may hold values from -4 to -1
Outputs:
- row_loss: float32 [32768], P(('group', 'blk')), parts along dimension 0
- image_grad: float32 [32768, 1152], P(('group', 'blk')), parts along dimension 0
- text_grad: float32 [32768, 1152], P(('group', 'blk')), parts along dimension 0
The draws below stay inside these ranges and needn't reach their ends.
There are 8 independent parts, one for each index of `group`. The reference program is written for one: setup_inputs(seed, part) draws one part's arguments, and reference() takes and returns one part's arrays. A program takes and returns all parts, laid end to end along the dimension named above; an argument that names none is the same for every part. Nothing has to cross between parts.
All inputs are finite; a program needn't handle non-finite values.
Results may differ from the reference program's by a relative error of at most 0.0085.
Values may be sent and summed in bfloat16 or wider, within the bound.
A program may use at most 128 MiB of HBM per device.

```python
import jax
import jax.numpy as jnp
from jax import lax

E = 1152
PAIRS = 4096


def pair_parts(key, common_weight):
    key_ids, key_signs, key_common, key_centers, key_own = jax.random.split(key, 5)
    cluster = jax.random.randint(key_ids, (PAIRS,), 0, 16)
    signs = (2 * jax.random.randint(key_signs, (16,), 0, 2) - 1).astype(jnp.float32)
    common = jax.random.normal(key_common, (E,), jnp.float32)
    spread_part = jax.random.normal(key_centers, (16, E), jnp.float32)
    centers = common_weight * signs[:, None] * common[None, :] + jnp.sqrt(jnp.float32(1.0 - common_weight * common_weight)) * spread_part
    base = centers[cluster]
    own = jax.random.normal(key_own, (PAIRS, E), jnp.float32)
    return (base, own)


def row_factors(key, spread):
    return jnp.exp(jax.random.uniform(key, (PAIRS, 1), jnp.float32, -spread, spread))


def draw_image_embed(key, part):
    base, own = pair_parts(key, 0.6)
    spread = 0.0
    key = jax.random.fold_in(key, 11)
    key_strength, key_factor = jax.random.split(key)
    strength = jax.random.uniform(key_strength, (PAIRS, 1), jnp.float32, 0.3, 1.0)
    values = 0.03 * row_factors(key_factor, spread) * (strength * base + own)
    return jnp.clip(values, -0.5, 0.5).astype(jnp.bfloat16)


def draw_text_embed(key, part):
    base, own = pair_parts(key, 0.6)
    spread = 0.0
    key = jax.random.fold_in(key, 23)
    key_strength, key_pull, key_noise, key_factor = jax.random.split(key, 4)
    strength = jax.random.uniform(key_strength, (PAIRS, 1), jnp.float32, 0.3, 1.0)
    pull = jax.random.uniform(key_pull, (PAIRS, 1), jnp.float32, 0.3, 0.9)
    noise = jax.random.normal(key_noise, (PAIRS, E), jnp.float32)
    values = 0.03 * row_factors(key_factor, spread) * (strength * base + pull * own + jnp.sqrt(1.0 - pull * pull) * noise)
    return jnp.clip(values, -0.5, 0.5).astype(jnp.bfloat16)


def setup_inputs(seed: int = 0, part: int = 0) -> dict:
    keys = jax.random.split(jax.random.key(seed), 5)
    own_keys = jax.random.split(jax.random.fold_in(keys[4], part), 5)
    image_embed = draw_image_embed(jax.random.fold_in(jax.random.fold_in(keys[4], part), 71), part)
    text_embed = draw_text_embed(jax.random.fold_in(jax.random.fold_in(keys[4], part), 71), part)
    logit_scale = jnp.clip(jax.random.uniform(keys[2], (1,), jnp.float32, 4.0, 12.0), 4.0, 12.0)
    logit_bias = jnp.clip(jax.random.uniform(keys[3], (1,), jnp.float32, -4.0, -1.0), -4.0, -1.0)
    return dict(image_embed=image_embed, text_embed=text_embed, logit_scale=logit_scale, logit_bias=logit_bias)


def normalize(rows_in):
    values = rows_in.astype(jnp.float32)
    norm = jnp.sqrt(lax.optimization_barrier(jnp.sum(values * values, axis=1, keepdims=True)) + 1e-06)
    return (values / norm, norm)

def unnormal(grad, unit, norm):
    return (grad - unit * lax.optimization_barrier(jnp.sum(unit * grad, axis=1, keepdims=True))) / norm

def reference(image_embed, text_embed, logit_scale, logit_bias):
    scale = logit_scale[0]
    bias = logit_bias[0]
    img_unit, img_norm = normalize(image_embed)
    txt_unit, txt_norm = normalize(text_embed)
    zi = img_unit.astype(jnp.bfloat16)
    zt = txt_unit.astype(jnp.bfloat16)
    logits = scale * lax.dot_general(zi, zt, (((1,), (1,)), ((), ())), preferred_element_type=jnp.float32) + bias
    count = logits.shape[0]
    rows_idx = lax.broadcasted_iota(jnp.int32, (count, count), 0)
    cols_idx = lax.broadcasted_iota(jnp.int32, (count, count), 1)
    sign = jnp.where(rows_idx == cols_idx, jnp.float32(1.0), jnp.float32(-1.0))
    row_loss = lax.optimization_barrier(jnp.sum(jax.nn.softplus(-sign * logits), axis=1))
    coef = (-sign * jax.nn.sigmoid(-sign * logits)).astype(jnp.bfloat16)
    g_img = scale * jnp.dot(coef, zt, preferred_element_type=jnp.float32)
    g_txt = scale * lax.dot_general(coef, zi, (((0,), (0,)), ((), ())), preferred_element_type=jnp.float32)
    return (row_loss, unnormal(g_img, img_unit, img_norm), unnormal(g_txt, txt_unit, txt_norm))
```

```python
import functools

import jax
import jax.numpy as jnp
from jax import lax
from jax.experimental import pallas as pl
from jax.experimental.pallas import tpu as pltpu
from jax.sharding import PartitionSpec as P

MESH = pl.DeviceIdType.MESH
F32 = jnp.float32
BF16 = jnp.bfloat16

RING = 8
QUAD = 4
RIGHT, LEFT = 0, 1
EPS = 1e-06
CODE = 2.0**13
TINY = 2.0**-126


def encode(x):
    a = x * CODE
    a2 = a * a
    return (a2 * a2 * a).astype(BF16)


def decode(y):
    y = y.astype(F32)
    root = jnp.exp(jnp.log(jnp.maximum(jnp.abs(y), TINY)) * 0.2) * (1.0 / CODE)
    return jnp.where(y < 0, -root, root)


def nt(a, b):
    return lax.dot_general(a, b, (((1,), (1,)), ((), ())), preferred_element_type=F32)


def tn(a, b):
    return lax.dot_general(a, b, (((0,), (0,)), ((), ())), preferred_element_type=F32)


def kernel(
    img_ref,
    txt_ref,
    scale_ref,
    bias_ref,
    loss_ref,
    gi_ref,
    gt_ref,
    img,
    txt,
    part,
    coefs,
    sums,
    rs_send,
    rs_recv,
    core_recv,
    y_recv,
    unit_i,
    unit_t,
    inv_i,
    inv_t,
    loss_part,
    loss_recv,
    ag_ssem,
    ag_rsem,
    rs_ssem,
    rs_rsem,
    loss_ssem,
    loss_rsem,
    t_ssem,
    t_rsem,
    c_ssem,
    c_rsem,
    y_ssem,
    y_rsem,
):
    rows = img_ref.shape[0]
    half = rows // 2
    sub = half // 2
    me = lax.axis_index("blk")
    n = RING * QUAD
    to = (lax.rem(me + QUAD, n), lax.rem(me + n - QUAD, n))
    other_core = me + 1 - 2 * lax.rem(me, 2)
    other_y = me + 2 - 4 * lax.rem(lax.div(me, 2), 2)

    def copy(src, dst, ssem, rsem, device):
        return pltpu.make_async_remote_copy(
            src_ref=src,
            dst_ref=dst,
            send_sem=ssem,
            recv_sem=rsem,
            device_id={"blk": device},
            device_id_type=MESH,
        )

    barrier = pltpu.get_barrier_semaphore()
    for peer in (*to, other_core, other_y):
        pl.semaphore_signal(barrier, inc=1, device_id={"blk": peer}, device_id_type=MESH)

    scale = scale_ref[0]
    bias = bias_ref[0]

    def normalize(src, at, size, unit, inv, out):
        values = src[pl.ds(at, size), :].astype(F32)
        norm = jnp.sqrt(jnp.sum(values * values, axis=1, keepdims=True) + EPS)
        inverse = 1.0 / norm
        u = values * inverse
        unit[pl.ds(at, size), :] = u
        inv[pl.ds(at, size), :] = jnp.broadcast_to(inverse, (size, 128))
        out[pl.ds(at, size), :] = u.astype(BF16)

    def gather(way, hop, piece):
        here = hop - 1 if way == RIGHT else lax.rem(RING + 1 - hop, RING)
        there = hop if way == RIGHT else RING - hop
        src = img.at[pl.ds(pl.multiple_of(here * rows + piece * half, half), half), :]
        dst = img.at[pl.ds(pl.multiple_of(there * rows + piece * half, half), half), :]
        at = (hop - 1) * 2 + piece
        return copy(src, dst, ag_ssem.at[way, at], ag_rsem.at[way, at], to[way])

    normalize(img_ref, 0, half, unit_i, inv_i, img)
    normalize(img_ref, half, half, unit_i, inv_i, img)
    pl.semaphore_wait(barrier, 4)
    gather(RIGHT, 1, 0).start()
    gather(LEFT, 1, 1).start()
    gather(RIGHT, 1, 1).start()
    gather(LEFT, 1, 0).start()

    normalize(txt_ref, 0, rows, unit_t, inv_t, txt)

    def text_copy(i):
        src = (0, 0, 2)[i]
        dst = (1, 2, 3)[i]
        device = (other_core, other_y, other_core)[i]
        return copy(
            txt.at[pl.ds(src * rows, rows), :],
            txt.at[pl.ds(dst * rows, rows), :],
            t_ssem.at[i],
            t_rsem.at[i],
            device,
        )

    text_copy(1).start()
    text_copy(0).start()

    def tile(slot, own):
        at = slot * rows if own else pl.multiple_of(slot * rows, rows)
        zi = img[pl.ds(at, rows), :]
        wide = 2 * rows
        total = jnp.zeros((rows, rows), F32)
        for h in range(2):
            m = nt(zi, txt[pl.ds(h * wide, wide), :]) * scale + bias
            if own and h == 0:
                eye = lax.broadcasted_iota(jnp.int32, m.shape, 0) == lax.broadcasted_iota(
                    jnp.int32, m.shape, 1
                )
                m = jnp.where(eye, -m, m)
            e = jnp.exp(-jnp.abs(m))
            soft = jnp.maximum(m, 0.0) + jnp.log1p(e)
            r = 1.0 / (1.0 + e)
            coef = jnp.where(m >= 0, r, e * r)
            if own and h == 0:
                coef = jnp.where(eye, -coef, coef)
            total = total + soft[:, :rows] + soft[:, rows:]
            coefs[pl.ds(at, rows), pl.ds(h * wide, wide)] = coef.astype(BF16)
        part[slot] = jnp.dot(coefs[pl.ds(at, rows), :], txt[...], preferred_element_type=F32)
        across = jnp.sum(total.T, axis=0, keepdims=True)
        loss_part[slot] = jnp.broadcast_to(across, (8, rows))

    def arrive(hop):
        for first in (True, False):
            for way in (RIGHT, LEFT):
                piece = (0 if first else 1) if way == RIGHT else (1 if first else 0)
                gather(way, hop, piece).wait_recv()
                if first:
                    gather(way, hop + 1, piece).start()
                else:

                    @pl.when(hop < 3)
                    def _():
                        gather(way, hop + 1, piece).start()

    def chunk(way, idx, s):
        src = rs_send.at[way, idx, pl.ds(pl.multiple_of(s * sub, sub), sub), :]
        dst = rs_recv.at[way, idx, pl.ds(pl.multiple_of(s * sub, sub), sub), :]
        at = idx * 2 + s
        return copy(src, dst, rs_ssem.at[way, at], rs_rsem.at[way, at], to[way])

    def late(way, j):
        slot = 4 + j if way == RIGHT else 4 - j
        return slot, (0 if way == RIGHT else half), j

    def early(way, j):
        slot = 5 + j if way == RIGHT else 3 - j
        return slot, (half if way == RIGHT else 0), 4 + j

    def pass_on(way, which, j):
        slot, row0, idx = which(way, j)

        def one(s, _):
            at = pl.multiple_of(s * sub, sub)
            x = part[slot, pl.ds(row0 + at, sub), :]
            if j > 0:
                chunk(way, idx - 1, s).wait_recv()
                x = x + decode(rs_recv[way, idx - 1, pl.ds(at, sub), :])
            rs_send[way, idx, pl.ds(at, sub), :] = encode(x)
            chunk(way, idx, s).start()
            return 0

        lax.fori_loop(0, 2, one, 0)

    def loss_copy(way, j):
        slot = 4 + j if way == RIGHT else 3 - j
        idx = j if way == RIGHT else 4 + j
        return copy(
            loss_part.at[slot], loss_recv.at[idx], loss_ssem.at[idx], loss_rsem.at[idx], to[way]
        )

    def loss_on(way, j):
        slot = 4 + j if way == RIGHT else 3 - j
        idx = j if way == RIGHT else 4 + j
        if j > 0:
            loss_copy(way, j - 1).wait_recv()
            loss_part[slot] += loss_recv[idx - 1]
        loss_copy(way, j).start()

    arrive(1)
    text_copy(1).wait_recv()
    text_copy(2).start()
    text_copy(0).wait_recv()
    text_copy(2).wait_recv()
    tile(0, True)

    def pair(hop):
        def one(way, _):
            tile(hop + way * (RING - 2 * hop), False)
            return 0

        lax.fori_loop(0, 2, one, 0)

    def hops(hop, _):
        @pl.when(hop > 1)
        def _():
            arrive(hop)

        pair(hop)
        return 0

    lax.fori_loop(1, 4, hops, 0)

    pass_on(RIGHT, early, 0)
    pass_on(LEFT, early, 0)
    gather(RIGHT, 4, 0).wait_recv()
    gather(LEFT, 4, 1).wait_recv()
    tile(4, False)
    pass_on(RIGHT, late, 0)
    pass_on(LEFT, late, 0)
    loss_on(RIGHT, 0)
    loss_on(LEFT, 0)

    def text_sums(b):
        sums[b] = tn(coefs[:, pl.ds(b * rows, rows)], img[...])

    def core_copy(i):
        return copy(sums.at[1 + 2 * i], core_recv.at[i], c_ssem.at[i], c_rsem.at[i], other_core)

    text_sums(3)
    core_copy(1).start()
    text_sums(1)
    core_copy(0).start()
    text_sums(2)
    text_sums(0)

    y_copy = copy(sums.at[2], y_recv, y_ssem.at[0], y_rsem.at[0], other_y)

    def step(j):
        if j < 3:
            pass_on(RIGHT, early, j)
            pass_on(LEFT, early, j)
        pass_on(RIGHT, late, j)
        pass_on(LEFT, late, j)
        loss_on(RIGHT, j)
        if j < 3:
            loss_on(LEFT, j)

    step(1)
    core_copy(1).wait_recv()
    sums[2] += core_recv[1]
    y_copy.start()
    core_copy(0).wait_recv()
    sums[0] += core_recv[0]
    step(2)
    step(3)

    def unnormal(g, unit, inv, at, size):
        u = unit[pl.ds(at, size), :]
        along = jnp.sum(u * g, axis=1, keepdims=True)
        return (g - u * along) * (inv[pl.ds(at, size), pl.ds(0, 1)] * scale)

    y_copy.wait_recv()

    def finish_text(i, _):
        at = pl.multiple_of(i * sub, sub)
        g = sums[0, pl.ds(at, sub), :] + y_recv[pl.ds(at, sub), :]
        gt_ref[pl.ds(at, sub), :] = unnormal(g, unit_t, inv_t, at, sub)
        return 0

    lax.fori_loop(0, 4, finish_text, 0)

    def finish(piece):
        idx = (3, 6) if piece == 0 else (6, 3)

        def one(s, _):
            at = pl.multiple_of(s * sub, sub)
            row = pl.multiple_of(piece * half + s * sub, sub)
            g = part[0, pl.ds(row, sub), :]
            for way in (RIGHT, LEFT):
                chunk(way, idx[way], s).wait_recv()
                g = g + decode(rs_recv[way, idx[way], pl.ds(at, sub), :])
            gi_ref[pl.ds(row, sub), :] = unnormal(g, unit_i, inv_i, row, sub)
            return 0

        lax.fori_loop(0, 2, one, 0)

    loss_copy(RIGHT, 3).wait_recv()
    loss_copy(LEFT, 2).wait_recv()
    loss_ref[...] = loss_part[0] + loss_recv[3] + loss_recv[6]
    finish(0)
    finish(1)

    for hop in range(1, 5):
        for way in (RIGHT, LEFT):
            for piece in (0, 1):
                if hop < 4 or piece == way:
                    gather(way, hop, piece).wait_send()
    for i in range(3):
        text_copy(i).wait_send()
    for i in range(2):
        core_copy(i).wait_send()
    y_copy.wait_send()
    for j in range(4):
        loss_copy(RIGHT, j).wait_send()
        if j < 3:
            loss_copy(LEFT, j).wait_send()
    for way in (RIGHT, LEFT):
        for idx in range(7):
            for s in range(2):
                chunk(way, idx, s).wait_send()


def per_device(image_embed, text_embed, logit_scale, logit_bias):
    rows, width = image_embed.shape
    half = rows // 2
    dma = pltpu.SemaphoreType.DMA
    vmem = pl.BlockSpec(memory_space=pltpu.VMEM)
    smem = pl.BlockSpec(memory_space=pltpu.SMEM)
    loss, image_grad, text_grad = pl.pallas_call(
        kernel,
        out_shape=(
            jax.ShapeDtypeStruct((8, rows), F32),
            jax.ShapeDtypeStruct((rows, width), F32),
            jax.ShapeDtypeStruct((rows, width), F32),
        ),
        in_specs=[vmem, vmem, smem, smem],
        out_specs=(vmem, vmem, vmem),
        scratch_shapes=[
            pltpu.VMEM((RING * rows, width), BF16),
            pltpu.VMEM((QUAD * rows, width), BF16),
            pltpu.VMEM((RING, rows, width), F32),
            pltpu.VMEM((RING * rows, QUAD * rows), BF16),
            pltpu.VMEM((QUAD, rows, width), F32),
            pltpu.VMEM((2, 7, half, width), BF16),
            pltpu.VMEM((2, 7, half, width), BF16),
            pltpu.VMEM((2, rows, width), F32),
            pltpu.VMEM((rows, width), F32),
            pltpu.VMEM((rows, width), F32),
            pltpu.VMEM((rows, width), F32),
            pltpu.VMEM((rows, 128), F32),
            pltpu.VMEM((rows, 128), F32),
            pltpu.VMEM((RING, 8, rows), F32),
            pltpu.VMEM((7, 8, rows), F32),
            dma((2, 8)),
            dma((2, 8)),
            dma((2, 14)),
            dma((2, 14)),
            dma((7,)),
            dma((7,)),
            dma((3,)),
            dma((3,)),
            dma((2,)),
            dma((2,)),
            dma((1,)),
            dma((1,)),
        ],
        compiler_params=pltpu.CompilerParams(
            collective_id=0, has_side_effects=True, vmem_limit_bytes=48 * 2**20
        ),
        cost_estimate=pl.CostEstimate(
            flops=3 * 2 * 1024 * 512 * width, bytes_accessed=6 * rows * width, transcendentals=0
        ),
    )(image_embed, text_embed, logit_scale, logit_bias)
    return loss[0], image_grad, text_grad


def solution(mesh):
    placed = (P(("group", "blk"), None), P(("group", "blk"), None), P(), P())
    return jax.shard_map(
        per_device,
        mesh=mesh,
        in_specs=placed,
        out_specs=(P(("group", "blk")), P(("group", "blk"), None), P(("group", "blk"), None)),
        check_vma=False,
    )
```

```python
import functools

import jax
import jax.numpy as jnp
from jax import lax
from jax.experimental import pallas as pl
from jax.experimental.pallas import tpu as pltpu
from jax.sharding import PartitionSpec as P

MESH = pl.DeviceIdType.MESH
F32 = jnp.float32
BF16 = jnp.bfloat16

RING = 8
QUAD = 4
RIGHT, LEFT = 0, 1
LATE, EARLY = 0, 1
EPS = 1e-06
CODE = 2.0**13
TINY = 2.0**-126


def encode(x):
    a = x * CODE
    a2 = a * a
    return (a2 * a2 * a).astype(BF16)


def decode(y):
    y = y.astype(F32)
    root = jnp.exp(jnp.log(jnp.maximum(jnp.abs(y), TINY)) * 0.2) * (1.0 / CODE)
    return jnp.where(y < 0, -root, root)


def nt(a, b):
    return lax.dot_general(a, b, (((1,), (1,)), ((), ())), preferred_element_type=F32)


def tn(a, b):
    return lax.dot_general(a, b, (((0,), (0,)), ((), ())), preferred_element_type=F32)


def kernel(
    img_hbm,
    txt_hbm,
    both_ref,
    loss_ref,
    gi_ref,
    gt_ref,
    img_ref,
    txt_ref,
    img,
    txt,
    part,
    coefs,
    sums,
    rs_send,
    rs_recv,
    core_recv,
    y_send,
    y_recv,
    unit_i,
    unit_t,
    inv_i,
    inv_t,
    loss_part,
    loss_send,
    loss_recv,
    in_sem,
    ag_ssem,
    ag_rsem,
    rs_ssem,
    rs_rsem,
    loss_ssem,
    loss_rsem,
    t_ssem,
    t_rsem,
    c_ssem,
    c_rsem,
    y_ssem,
    y_rsem,
):
    rows = img_ref.shape[0]
    half = rows // 2
    sub = half // 2
    me = lax.axis_index("blk")
    n = RING * QUAD
    to = (lax.rem(me + QUAD, n), lax.rem(me + n - QUAD, n))
    other_core = me + 1 - 2 * lax.rem(me, 2)
    other_y = me + 2 - 4 * lax.rem(lax.div(me, 2), 2)

    def copy(src, dst, ssem, rsem, device):
        return pltpu.make_async_remote_copy(
            src_ref=src,
            dst_ref=dst,
            send_sem=ssem,
            recv_sem=rsem,
            device_id={"blk": device},
            device_id_type=MESH,
        )

    barrier = pltpu.get_barrier_semaphore()
    for peer in (*to, other_core, other_y):
        pl.semaphore_signal(barrier, inc=1, device_id={"blk": peer}, device_id_type=MESH)

    def load(i):
        src, dst = ((img_hbm, img_ref), (txt_hbm, txt_ref))[i // 2]
        some = pl.ds(i % 2 * half, half)
        return pltpu.make_async_copy(src.at[some, :], dst.at[some, :], in_sem.at[i])

    for i in range(4):
        load(i).start()

    def normalize(src, at, size, unit, inv, out):
        values = src[pl.ds(at, size), :].astype(F32)
        norm = jnp.sqrt(jnp.sum(values * values, axis=1, keepdims=True) + EPS)
        inverse = 1.0 / norm
        u = values * inverse
        unit[pl.ds(at, size), :] = u
        inv[pl.ds(at, size), :] = jnp.broadcast_to(inverse, (size, 128))
        out[pl.ds(at, size), :] = u.astype(BF16)

    def place(way, i, s):
        side = way if i < 6 else 1 - way
        return s * half + side * sub

    def gather(way, i, s):
        if i < 2:
            piece = i if way == RIGHT else 1 - i
            src = img.at[0, pl.ds(piece * half + s * sub, sub), :]
        else:
            src = img.at[i - 1, pl.ds(place(way, i - 2, s), sub), :]
        dst = img.at[i + 1, pl.ds(place(way, i, s), sub), :]
        return copy(src, dst, ag_ssem.at[way, i, s], ag_rsem.at[way, i, s], to[way])

    for i in range(2):
        load(i).wait()
        normalize(img_ref, i * half, half, unit_i, inv_i, img.at[0])
    pl.semaphore_wait(barrier, 4)
    for i in range(2):
        for s in range(2):
            for way in (RIGHT, LEFT):
                gather(way, i, s).start()

    for i in range(2):
        load(2 + i).wait()
        normalize(txt_ref, i * half, half, unit_t, inv_t, txt)

    scale = both_ref[0:1, 0:1]
    bias = both_ref[1:2, 0:1]

    def text_copy(i):
        src = (0, 0, 2)[i]
        dst = (1, 2, 3)[i]
        device = (other_core, other_y, other_core)[i]
        return copy(
            txt.at[pl.ds(src * rows, rows), :],
            txt.at[pl.ds(dst * rows, rows), :],
            t_ssem.at[i],
            t_rsem.at[i],
            device,
        )

    text_copy(1).start()
    text_copy(0).start()

    def tile(block, at, size, own=False):
        some = pl.ds(at, size)
        wide = 2 * rows
        total = jnp.zeros((size, rows), F32)
        for h in range(2):
            m = nt(img[block, some, :], txt[pl.ds(h * wide, wide), :]) * scale + bias
            if own and h == 0:
                eye = lax.broadcasted_iota(jnp.int32, m.shape, 0) == lax.broadcasted_iota(
                    jnp.int32, m.shape, 1
                )
                m = jnp.where(eye, -m, m)
            e = jnp.exp(-jnp.abs(m))
            soft = jnp.maximum(m, 0.0) + jnp.log1p(e)
            r = 1.0 / (1.0 + e)
            coef = jnp.where(m >= 0, r, e * r)
            if own and h == 0:
                coef = jnp.where(eye, -coef, coef)
            total = total + soft[:, :rows] + soft[:, rows:]
            coefs[block, some, pl.ds(h * wide, wide)] = coef.astype(BF16)
        part[block, some, :] = jnp.dot(
            coefs[block, some, :], txt[...], preferred_element_type=F32
        )
        if size < rows:
            total = jnp.concatenate([total, total], axis=0)
        across = jnp.broadcast_to(jnp.sum(total.T, axis=0, keepdims=True), (8, rows))
        if size < rows and at > 0:
            lane = lax.broadcasted_iota(jnp.int32, (8, rows), 1)
            across = jnp.where(lane < at, loss_part[block], across)
        loss_part[block] = across

    def serve(i, s):
        for way in (RIGHT, LEFT):
            gather(way, i, s).wait_recv()
            if i < 5:
                gather(way, i + 2, s).start()

    def block_of(kind, j):
        return (7, 6, 4, 2)[j] if kind == LATE else (5, 3, 1)[j]

    def chunk(way, kind, j, s):
        at = 4 * kind + j
        some = pl.ds(s * sub, sub)
        return copy(
            rs_send.at[way, at, some, :],
            rs_recv.at[way, at, some, :],
            rs_ssem.at[way, at, s],
            rs_rsem.at[way, at, s],
            to[way],
        )

    def pass_on(kind, j, s):
        block = block_of(kind, j)
        for way in (RIGHT, LEFT):
            some = pl.ds(s * half + (1 - way) * sub, sub)
            x = part[block, some, :]
            if j > 0:
                chunk(way, kind, j - 1, s).wait_recv()
                x = x + decode(rs_recv[way, 4 * kind + j - 1, pl.ds(s * sub, sub), :])
            rs_send[way, 4 * kind + j, pl.ds(s * sub, sub), :] = encode(x)
            chunk(way, kind, j, s).start()

    def loss_copy(way, kind, j):
        at = 4 * kind + j
        return copy(
            loss_send.at[way, at],
            loss_recv.at[way, at],
            loss_ssem.at[way, at],
            loss_rsem.at[way, at],
            to[way],
        )

    def loss_on(kind, j):
        for way in (RIGHT, LEFT):
            x = loss_part[block_of(kind, j)]
            if j > 0:
                loss_copy(way, kind, j - 1).wait_recv()
                x = x + loss_recv[way, 4 * kind + j - 1]
            loss_send[way, 4 * kind + j] = x
            loss_copy(way, kind, j).start()

    def both_subs(f, *args):
        for s in range(2):
            f(*args, s)

    both_subs(serve, 0)
    both_subs(serve, 1)
    text_copy(1).wait_recv()
    text_copy(2).start()
    both_subs(serve, 2)
    text_copy(0).wait_recv()
    text_copy(2).wait_recv()
    tile(0, 0, rows, True)

    def some_tiles(first, count):
        def one(block, _):
            tile(block, 0, rows)
            return 0

        lax.fori_loop(first, first + count, one, 0)

    some_tiles(1, 2)
    both_subs(serve, 3)
    some_tiles(3, 2)
    both_subs(serve, 4)
    some_tiles(5, 1)
    both_subs(pass_on, EARLY, 0)
    loss_on(EARLY, 0)
    both_subs(serve, 5)
    some_tiles(6, 1)
    for s in range(2):
        serve(6, s)
        tile(7, s * half, half)
        pass_on(LATE, 0, s)
    loss_on(LATE, 0)

    def text_sums(b):
        sums[b] = tn(
            coefs[:, :, pl.ds(b * rows, rows)].reshape(RING * rows, rows),
            img[...].reshape(RING * rows, img.shape[2]),
        )

    def core_copy(i):
        return copy(sums.at[1 + 2 * i], core_recv.at[i], c_ssem.at[i], c_rsem.at[i], other_core)

    y_copy = copy(y_send, y_recv, y_ssem.at[0], y_rsem.at[0], other_y)

    text_sums(3)
    core_copy(1).start()
    text_sums(1)
    core_copy(0).start()
    both_subs(pass_on, EARLY, 1)
    loss_on(EARLY, 1)
    text_sums(2)
    text_sums(0)
    both_subs(pass_on, LATE, 1)
    loss_on(LATE, 1)
    core_copy(1).wait_recv()
    y_send[...] = encode(sums[2] + core_recv[1])
    y_copy.start()
    pass_on(EARLY, 2, 0)
    loss_on(EARLY, 2)
    both_subs(pass_on, LATE, 2)
    loss_on(LATE, 2)
    pass_on(EARLY, 2, 1)
    core_copy(0).wait_recv()
    sums[0] += core_recv[0]
    loss_on(LATE, 3)
    both_subs(pass_on, LATE, 3)

    def unnormal(g, unit, inv, at, size):
        u = unit[pl.ds(at, size), :]
        along = jnp.sum(u * g, axis=1, keepdims=True)
        return (g - u * along) * (inv[pl.ds(at, size), pl.ds(0, 1)] * scale)

    def row_of(way, kind, s):
        return (half if (way == RIGHT) == (kind == EARLY) else 0) + s * sub

    def last(way, kind, s):
        chunk(way, kind, 3 - kind, s).wait_recv()
        return decode(rs_recv[way, 4 * kind + 3 - kind, pl.ds(s * sub, sub), :])

    for s in range(2):
        for way in (RIGHT, LEFT):
            some = pl.ds(row_of(way, EARLY, s), sub)
            part[0, some, :] += last(way, EARLY, s)

    y_copy.wait_recv()

    def finish_text(i, _):
        at = pl.multiple_of(i * sub, sub)
        g = sums[0, pl.ds(at, sub), :] + decode(y_recv[pl.ds(at, sub), :])
        gt_ref[pl.ds(at, sub), :] = unnormal(g, unit_t, inv_t, at, sub)
        return 0

    lax.fori_loop(0, 4, finish_text, 0)

    def lanes(way, kind):
        loss_copy(way, kind, 3 - kind).wait_recv()
        x = loss_recv[way, 4 * kind + 3 - kind]
        at = (1 - way) * sub
        return [x[:, s * half + at : s * half + at + sub] for s in range(2)]

    loss_ref[...] = (
        loss_part[0]
        + jnp.concatenate(lanes(RIGHT, LATE) + lanes(RIGHT, EARLY), axis=1)
        + jnp.concatenate(lanes(LEFT, EARLY) + lanes(LEFT, LATE), axis=1)
    )
    for s in range(2):
        for way in (RIGHT, LEFT):
            at = row_of(way, LATE, s)
            g = part[0, pl.ds(at, sub), :] + last(way, LATE, s)
            gi_ref[pl.ds(at, sub), :] = unnormal(g, unit_i, inv_i, at, sub)

    for way in (RIGHT, LEFT):
        for i in range(7):
            kind, j = i // 4, i % 4
            for s in range(2):
                gather(way, i, s).wait_send()
                chunk(way, kind, j, s).wait_send()
            loss_copy(way, kind, j).wait_send()
    for i in range(3):
        text_copy(i).wait_send()
    for i in range(2):
        core_copy(i).wait_send()
    y_copy.wait_send()


def write_out(loss_in, gi_in, gt_in, loss_out, gi_out, gt_out, sem):
    some = gi_in.shape[0] // 4
    copies = [
        pltpu.make_async_copy(
            src.at[pl.ds(i * some, some), :], dst.at[pl.ds(i * some, some), :], sem.at[k, i]
        )
        for i in range(4)
        for k, (src, dst) in enumerate(((gi_in, gi_out), (gt_in, gt_out)))
    ]
    for c in copies:
        c.start()
    loss_out[...] = loss_in[0]
    for c in copies:
        c.wait()


def per_device(image_embed, text_embed, logit_scale, logit_bias):
    rows, width = image_embed.shape
    half = rows // 2
    dma = pltpu.SemaphoreType.DMA
    vmem = pl.BlockSpec(memory_space=pltpu.VMEM)
    hbm = pl.BlockSpec(memory_space=pltpu.HBM)
    image_embed = pltpu.with_memory_space_constraint(image_embed, pltpu.HBM)
    text_embed = pltpu.with_memory_space_constraint(text_embed, pltpu.HBM)
    row = lax.broadcasted_iota(jnp.int32, (8, 128), 0)
    both = jnp.where(row == 0, logit_scale[0], logit_bias[0])
    anywhere = pl.BlockSpec(memory_space=pl.ANY)
    results = pl.pallas_call(
        kernel,
        out_shape=(
            pltpu.VMEM((8, rows), F32),
            pltpu.VMEM((rows, width), F32),
            pltpu.VMEM((rows, width), F32),
        ),
        in_specs=[hbm, hbm, vmem],
        out_specs=(vmem, vmem, vmem),
        scratch_shapes=[
            pltpu.VMEM((rows, width), BF16),
            pltpu.VMEM((rows, width), BF16),
            pltpu.VMEM((RING, rows, width), BF16),
            pltpu.VMEM((QUAD * rows, width), BF16),
            pltpu.VMEM((RING, rows, width), F32),
            pltpu.VMEM((RING, rows, QUAD * rows), BF16),
            pltpu.VMEM((QUAD, rows, width), F32),
            pltpu.VMEM((2, 7, half, width), BF16),
            pltpu.VMEM((2, 7, half, width), BF16),
            pltpu.VMEM((2, rows, width), F32),
            pltpu.VMEM((rows, width), BF16),
            pltpu.VMEM((rows, width), BF16),
            pltpu.VMEM((rows, width), F32),
            pltpu.VMEM((rows, width), F32),
            pltpu.VMEM((rows, 128), F32),
            pltpu.VMEM((rows, 128), F32),
            pltpu.VMEM((RING, 8, rows), F32),
            pltpu.VMEM((2, 7, 8, rows), F32),
            pltpu.VMEM((2, 7, 8, rows), F32),
            dma((4,)),
            dma((2, 7, 2)),
            dma((2, 7, 2)),
            dma((2, 7, 2)),
            dma((2, 7, 2)),
            dma((2, 7)),
            dma((2, 7)),
            dma((3,)),
            dma((3,)),
            dma((2,)),
            dma((2,)),
            dma((1,)),
            dma((1,)),
        ],
        compiler_params=pltpu.CompilerParams(
            collective_id=0, has_side_effects=True, vmem_limit_bytes=48 * 2**20
        ),
        cost_estimate=pl.CostEstimate(
            flops=3 * 2 * 1024 * 512 * width, bytes_accessed=6 * rows * width, transcendentals=0
        ),
    )(image_embed, text_embed, both)
    return pl.pallas_call(
        write_out,
        out_shape=(
            jax.ShapeDtypeStruct((rows,), F32),
            jax.ShapeDtypeStruct((rows, width), F32),
            jax.ShapeDtypeStruct((rows, width), F32),
        ),
        in_specs=[vmem, vmem, vmem],
        out_specs=(vmem, anywhere, anywhere),
        scratch_shapes=[dma((2, 4))],
        compiler_params=pltpu.CompilerParams(vmem_limit_bytes=2**20),
        cost_estimate=pl.CostEstimate(flops=0, bytes_accessed=16 * rows * width, transcendentals=0),
    )(*results)


def solution(mesh):
    placed = (P(("group", "blk"), None), P(("group", "blk"), None), P(), P())
    return jax.shard_map(
        per_device,
        mesh=mesh,
        in_specs=placed,
        out_specs=(P(("group", "blk")), P(("group", "blk"), None), P(("group", "blk"), None)),
        check_vma=False,
    )
```

```python
import functools

import jax
import jax.numpy as jnp
from jax import lax
from jax.experimental import pallas as pl
from jax.experimental.pallas import tpu as pltpu
from jax.sharding import PartitionSpec as P

MESH = pl.DeviceIdType.MESH
F32 = jnp.float32
BF16 = jnp.bfloat16

RING = 8
QUAD = 4
RIGHT, LEFT = 0, 1
LATE, EARLY = 0, 1
EPS = 1e-06
CODE = 2.0**13
TINY = 2.0**-126


def encode(x):
    a = x * CODE
    a2 = a * a
    return (a2 * a2 * a).astype(BF16)


def decode(y):
    y = y.astype(F32)
    root = jnp.exp(jnp.log(jnp.maximum(jnp.abs(y), TINY)) * 0.2) * (1.0 / CODE)
    return jnp.where(y < 0, -root, root)


def nt(a, b):
    return lax.dot_general(a, b, (((1,), (1,)), ((), ())), preferred_element_type=F32)


def tn(a, b):
    return lax.dot_general(a, b, (((0,), (0,)), ((), ())), preferred_element_type=F32)


def kernel(
    img_hbm,
    txt_hbm,
    both_ref,
    loss_ref,
    gi_ref,
    gt_ref,
    img_ref,
    txt_ref,
    img,
    txt,
    part,
    coefs,
    sums,
    rs_send,
    rs_recv,
    core_recv,
    y_send,
    y_recv,
    unit_i,
    unit_t,
    inv_i,
    inv_t,
    loss_part,
    loss_send,
    loss_recv,
    in_sem,
    ag_ssem,
    ag_rsem,
    rs_ssem,
    rs_rsem,
    loss_ssem,
    loss_rsem,
    t_ssem,
    t_rsem,
    c_ssem,
    c_rsem,
    y_ssem,
    y_rsem,
):
    rows = img_ref.shape[0]
    half = rows // 2
    sub = half // 2
    me = lax.axis_index("blk")
    n = RING * QUAD
    to = (lax.rem(me + QUAD, n), lax.rem(me + n - QUAD, n))
    other_core = me + 1 - 2 * lax.rem(me, 2)
    other_y = me + 2 - 4 * lax.rem(lax.div(me, 2), 2)

    def copy(src, dst, ssem, rsem, device):
        return pltpu.make_async_remote_copy(
            src_ref=src,
            dst_ref=dst,
            send_sem=ssem,
            recv_sem=rsem,
            device_id={"blk": device},
            device_id_type=MESH,
        )

    barrier = pltpu.get_barrier_semaphore()
    for peer in (*to, other_core, other_y):
        pl.semaphore_signal(barrier, inc=1, device_id={"blk": peer}, device_id_type=MESH)

    def load(i):
        src, dst = ((img_hbm, img_ref), (txt_hbm, txt_ref))[i // 2]
        some = pl.ds(i % 2 * half, half)
        return pltpu.make_async_copy(src.at[some, :], dst.at[some, :], in_sem.at[i])

    for i in range(4):
        load(i).start()

    def normalize(src, at, size, unit, inv, out):
        values = src[pl.ds(at, size), :].astype(F32)
        norm = jnp.sqrt(jnp.sum(values * values, axis=1, keepdims=True) + EPS)
        inverse = 1.0 / norm
        u = values * inverse
        unit[pl.ds(at, size), :] = u
        inv[pl.ds(at, size), :] = jnp.broadcast_to(inverse, (size, 128))
        out[pl.ds(at, size), :] = u.astype(BF16)

    def place(way, i, s):
        side = way if i < 6 else 1 - way
        return s * half + side * sub

    def gather(way, i, s):
        if i < 2:
            piece = i if way == RIGHT else 1 - i
            src = img.at[0, pl.ds(piece * half + s * sub, sub), :]
        else:
            src = img.at[i - 1, pl.ds(place(way, i - 2, s), sub), :]
        dst = img.at[i + 1, pl.ds(place(way, i, s), sub), :]
        return copy(src, dst, ag_ssem.at[way, i, s], ag_rsem.at[way, i, s], to[way])

    for i in range(2):
        load(i).wait()
        normalize(img_ref, i * half, half, unit_i, inv_i, img.at[0])
        if i == 0:
            pl.semaphore_wait(barrier, 4)
        for s in range(2):
            gather(i, 0, s).start()
    for s in range(2):
        for way in (RIGHT, LEFT):
            gather(way, 1, s).start()

    for i in range(2):
        load(2 + i).wait()
        normalize(txt_ref, i * half, half, unit_t, inv_t, txt)

    scale = both_ref[0:1, 0:1]
    bias = both_ref[1:2, 0:1]

    def text_copy(i):
        src = (0, 0, 2)[i]
        dst = (1, 2, 3)[i]
        device = (other_core, other_y, other_core)[i]
        return copy(
            txt.at[pl.ds(src * rows, rows), :],
            txt.at[pl.ds(dst * rows, rows), :],
            t_ssem.at[i],
            t_rsem.at[i],
            device,
        )

    text_copy(1).start()
    text_copy(0).start()

    def tile(block, at, size, maybe_own=False):
        some = pl.ds(at, size)
        wide = 2 * rows
        total = jnp.zeros((size, rows), F32)
        for h in range(2):
            m = nt(img[block, some, :], txt[pl.ds(h * wide, wide), :]) * scale + bias
            if maybe_own and h == 0:
                row = lax.broadcasted_iota(jnp.int32, m.shape, 0)
                col = lax.broadcasted_iota(jnp.int32, m.shape, 1)
                eye = row + jnp.where(block == 0, 0, 2 * wide) == col
                m = jnp.where(eye, -m, m)
            e = jnp.exp(-jnp.abs(m))
            soft = jnp.maximum(m, 0.0) + jnp.log1p(e)
            r = 1.0 / (1.0 + e)
            coef = jnp.where(m >= 0, r, e * r)
            if maybe_own and h == 0:
                coef = jnp.where(eye, -coef, coef)
            total = total + soft[:, :rows] + soft[:, rows:]
            coefs[block, some, pl.ds(h * wide, wide)] = coef.astype(BF16)
        part[block, some, :] = jnp.dot(
            coefs[block, some, :], txt[...], preferred_element_type=F32
        )
        if size < rows:
            total = jnp.concatenate([total, total], axis=0)
        across = jnp.broadcast_to(jnp.sum(total.T, axis=0, keepdims=True), (8, rows))
        if size < rows:
            lane = lax.broadcasted_iota(jnp.int32, (8, rows), 1)
            across = jnp.where(lane < at, loss_part[block], across)
        loss_part[block] = across

    def serve(i, s):
        for way in (RIGHT, LEFT):
            gather(way, i, s).wait_recv()
            if i < 5:
                gather(way, i + 2, s).start()

    def gather_wait(way, i, s):
        row = pl.multiple_of(place(way, i, s), sub)
        some = img.at[i + 1, pl.ds(row, sub), :]
        copy(some, some, ag_ssem.at[way, i, s], ag_rsem.at[way, i, s], to[way]).wait_recv()

    def block_of(kind, j):
        return (7, 6, 4, 2)[j] if kind == LATE else (5, 3, 1)[j]

    def chunk(way, kind, j, s):
        at = 4 * kind + j
        some = pl.ds(pl.multiple_of(s * sub, sub), sub)
        return copy(
            rs_send.at[way, at, some, :],
            rs_recv.at[way, at, some, :],
            rs_ssem.at[way, at, s],
            rs_rsem.at[way, at, s],
            to[way],
        )

    def pass_on(kind, j, first=0, count=2):
        def one(s, _):
            some = pl.ds(pl.multiple_of(s * sub, sub), sub)
            for way in (RIGHT, LEFT):
                row = pl.multiple_of(s * half + (1 - way) * sub, sub)
                x = part[block_of(kind, j), pl.ds(row, sub), :]
                if j > 0:
                    chunk(way, kind, j - 1, s).wait_recv()
                    x = x + decode(rs_recv[way, 4 * kind + j - 1, some, :])
                rs_send[way, 4 * kind + j, some, :] = encode(x)
                chunk(way, kind, j, s).start()
            return 0

        lax.fori_loop(first, first + count, one, 0)

    def loss_copy(way, kind, j):
        at = 4 * kind + j
        return copy(
            loss_send.at[way, at],
            loss_recv.at[way, at],
            loss_ssem.at[way, at],
            loss_rsem.at[way, at],
            to[way],
        )

    def loss_on(kind, j):
        for way in (RIGHT, LEFT):
            x = loss_part[block_of(kind, j)]
            if j > 0:
                loss_copy(way, kind, j - 1).wait_recv()
                x = x + loss_recv[way, 4 * kind + j - 1]
            loss_send[way, 4 * kind + j] = x
            loss_copy(way, kind, j).start()

    for i in range(2):
        serve(i, 0)
        serve(i, 1)
    text_copy(1).wait_recv()
    text_copy(2).start()
    serve(2, 0)
    serve(2, 1)
    text_copy(0).wait_recv()
    text_copy(2).wait_recv()

    def work(k, _):
        @pl.when(k == 1)
        def _():
            serve(3, 0)

        @pl.when(k == 2)
        def _():
            serve(3, 1)

        @pl.when(k == 4)
        def _():
            serve(4, 0)
            serve(4, 1)

        @pl.when(k == 5)
        def _():
            loss_on(EARLY, 0)
            pass_on(EARLY, 0)

        @pl.when(k == 6)
        def _():
            serve(5, 0)
            serve(5, 1)

        tile(jnp.where(k < 5, k + 1, jnp.where(k == 5, 0, 6)), 0, rows, True)
        return 0

    lax.fori_loop(0, 7, work, 0)

    def farthest(s, _):
        for way in (RIGHT, LEFT):
            gather_wait(way, 6, s)
        tile(7, pl.multiple_of(s * half, half), half)
        pl.when(s == 1)(lambda: loss_on(LATE, 0))
        pass_on(LATE, 0, s, 1)
        return 0

    lax.fori_loop(0, 2, farthest, 0)

    def text_sums(b):
        sums[b] = tn(
            coefs[:, :, pl.ds(pl.multiple_of(b * rows, rows), rows)].reshape(RING * rows, rows),
            img[...].reshape(RING * rows, img.shape[2]),
        )

    def core_copy(i):
        return copy(sums.at[1 + 2 * i], core_recv.at[i], c_ssem.at[i], c_rsem.at[i], other_core)

    y_copy = copy(y_send, y_recv, y_ssem.at[0], y_rsem.at[0], other_y)

    def sums_work(k, _):
        b = jnp.where(k == 0, 3, jnp.where(k == 1, 1, jnp.where(k == 2, 2, 0)))
        text_sums(b)

        @pl.when(k == 0)
        def _():
            core_copy(1).start()

        @pl.when(k == 1)
        def _():
            core_copy(0).start()
            loss_on(EARLY, 1)
            pass_on(EARLY, 1)

        return 0

    lax.fori_loop(0, QUAD, sums_work, 0)
    loss_on(LATE, 1)
    pass_on(LATE, 1)
    core_copy(1).wait_recv()
    y_send[...] = encode(sums[2] + core_recv[1])
    y_copy.start()
    loss_on(EARLY, 2)
    pass_on(EARLY, 2, 0, 1)
    loss_on(LATE, 2)
    pass_on(LATE, 2)
    pass_on(EARLY, 2, 1, 1)
    core_copy(0).wait_recv()
    sums[0] += core_recv[0]
    loss_on(LATE, 3)
    pass_on(LATE, 3)

    def sent(i, _):
        for way in (RIGHT, LEFT):
            for s in range(2):
                some = img.at[i, pl.ds(s * sub, sub), :]
                copy(some, some, ag_ssem.at[way, i, s], ag_rsem.at[way, i, s], to[way]).wait_send()
        return 0

    lax.fori_loop(0, 7, sent, 0)
    for i in range(3):
        text_copy(i).wait_send()
    for i in range(2):
        core_copy(i).wait_send()

    def summed(at):
        for way in (RIGHT, LEFT):
            for s in range(2):
                some = rs_send.at[way, at, pl.ds(s * sub, sub), :]
                copy(some, some, rs_ssem.at[way, at, s], rs_rsem.at[way, at, s], to[way]).wait_send()
            x = loss_send.at[way, at]
            copy(x, x, loss_ssem.at[way, at], loss_rsem.at[way, at], to[way]).wait_send()

    lax.fori_loop(0, 3, lambda i, _: (summed(i), 0)[1], 0)
    lax.fori_loop(4, 7, lambda i, _: (summed(i), 0)[1], 0)

    def unnormal(g, u, inv):
        along = jnp.sum(u * g, axis=1, keepdims=True)
        return (g - u * along) * (inv[:, 0:1] * scale)

    def last(way, kind, s):
        some = pl.ds(pl.multiple_of(s * sub, sub), sub)
        chunk(way, kind, 3 - kind, s).wait_recv()
        at = (half if (way == RIGHT) == (kind == EARLY) else 0) + s * sub
        at = pl.ds(pl.multiple_of(at, sub), sub)
        return at, part[0, at, :] + decode(rs_recv[way, 4 * kind + 3 - kind, some, :])

    def add_early(s, _):
        for way in (RIGHT, LEFT):
            at, x = last(way, EARLY, s)
            part[0, at, :] = x
        return 0

    lax.fori_loop(0, 2, add_early, 0)
    y_copy.wait_recv()

    def finish_text(i, _):
        at = pl.ds(pl.multiple_of(i * sub, sub), sub)
        g = sums[0, at, :] + decode(y_recv[at, :])
        gt_ref[at, :] = unnormal(g, unit_t[at, :], inv_t[at, :])
        return 0

    lax.fori_loop(0, 4, finish_text, 0)

    def lanes(way, kind):
        loss_copy(way, kind, 3 - kind).wait_recv()
        x = loss_recv[way, 4 * kind + 3 - kind]
        at = (1 - way) * sub
        return [x[:, s * half + at : s * half + at + sub] for s in range(2)]

    loss_ref[...] = (
        loss_part[0]
        + jnp.concatenate(lanes(RIGHT, LATE) + lanes(RIGHT, EARLY), axis=1)
        + jnp.concatenate(lanes(LEFT, EARLY) + lanes(LEFT, LATE), axis=1)
    )
    y_copy.wait_send()

    def finish(s, _):
        for way in (RIGHT, LEFT):
            at, g = last(way, LATE, s)
            gi_ref[at, :] = unnormal(g, unit_i[at, :], inv_i[at, :])
        return 0

    lax.fori_loop(0, 2, finish, 0)
    summed(3)


def write_out(loss_in, gi_in, gt_in, loss_out, gi_out, gt_out, row, sem):
    copies = [
        pltpu.make_async_copy(gi_in, gi_out, sem.at[0]),
        pltpu.make_async_copy(gt_in, gt_out, sem.at[1]),
        pltpu.make_async_copy(row, loss_out, sem.at[2]),
    ]
    row[...] = loss_in[0]
    for c in copies:
        c.start()
    for c in copies:
        c.wait()


def per_device(image_embed, text_embed, logit_scale, logit_bias):
    rows, width = image_embed.shape
    half = rows // 2
    dma = pltpu.SemaphoreType.DMA
    vmem = pl.BlockSpec(memory_space=pltpu.VMEM)
    hbm = pl.BlockSpec(memory_space=pltpu.HBM)
    image_embed = pltpu.with_memory_space_constraint(image_embed, pltpu.HBM)
    text_embed = pltpu.with_memory_space_constraint(text_embed, pltpu.HBM)
    row = lax.broadcasted_iota(jnp.int32, (8, 128), 0)
    both = jnp.where(row == 0, logit_scale[0], logit_bias[0])
    anywhere = pl.BlockSpec(memory_space=pl.ANY)
    results = pl.pallas_call(
        kernel,
        out_shape=(
            pltpu.VMEM((8, rows), F32),
            pltpu.VMEM((rows, width), F32),
            pltpu.VMEM((rows, width), F32),
        ),
        in_specs=[hbm, hbm, vmem],
        out_specs=(vmem, vmem, vmem),
        scratch_shapes=[
            pltpu.VMEM((rows, width), BF16),
            pltpu.VMEM((rows, width), BF16),
            pltpu.VMEM((RING, rows, width), BF16),
            pltpu.VMEM((QUAD * rows, width), BF16),
            pltpu.VMEM((RING, rows, width), F32),
            pltpu.VMEM((RING, rows, QUAD * rows), BF16),
            pltpu.VMEM((QUAD, rows, width), F32),
            pltpu.VMEM((2, 7, half, width), BF16),
            pltpu.VMEM((2, 7, half, width), BF16),
            pltpu.VMEM((2, rows, width), F32),
            pltpu.VMEM((rows, width), BF16),
            pltpu.VMEM((rows, width), BF16),
            pltpu.VMEM((rows, width), F32),
            pltpu.VMEM((rows, width), F32),
            pltpu.VMEM((rows, 128), F32),
            pltpu.VMEM((rows, 128), F32),
            pltpu.VMEM((RING, 8, rows), F32),
            pltpu.VMEM((2, 7, 8, rows), F32),
            pltpu.VMEM((2, 7, 8, rows), F32),
            dma((4,)),
            dma((2, 7, 2)),
            dma((2, 7, 2)),
            dma((2, 7, 2)),
            dma((2, 7, 2)),
            dma((2, 7)),
            dma((2, 7)),
            dma((3,)),
            dma((3,)),
            dma((2,)),
            dma((2,)),
            dma((1,)),
            dma((1,)),
        ],
        compiler_params=pltpu.CompilerParams(
            collective_id=0, has_side_effects=True, vmem_limit_bytes=48 * 2**20
        ),
        cost_estimate=pl.CostEstimate(
            flops=3 * 2 * 1024 * 512 * width, bytes_accessed=6 * rows * width, transcendentals=0
        ),
    )(image_embed, text_embed, both)
    return pl.pallas_call(
        write_out,
        out_shape=(
            jax.ShapeDtypeStruct((rows,), F32),
            jax.ShapeDtypeStruct((rows, width), F32),
            jax.ShapeDtypeStruct((rows, width), F32),
        ),
        in_specs=[vmem, vmem, vmem],
        out_specs=(anywhere, anywhere, anywhere),
        scratch_shapes=[pltpu.VMEM((rows,), F32), dma((3,))],
        compiler_params=pltpu.CompilerParams(vmem_limit_bytes=2**20),
        cost_estimate=pl.CostEstimate(flops=0, bytes_accessed=16 * rows * width, transcendentals=0),
    )(*results)


def solution(mesh):
    placed = (P(("group", "blk"), None), P(("group", "blk"), None), P(), P())
    return jax.shard_map(
        per_device,
        mesh=mesh,
        in_specs=placed,
        out_specs=(P(("group", "blk")), P(("group", "blk"), None), P(("group", "blk"), None)),
        check_vma=False,
    )
```

```python
import functools

import jax
import jax.numpy as jnp
from jax import lax
from jax.experimental import pallas as pl
from jax.experimental.pallas import tpu as pltpu
from jax.sharding import PartitionSpec as P

MESH = pl.DeviceIdType.MESH
F32 = jnp.float32
BF16 = jnp.bfloat16

RING = 8
QUAD = 4
RIGHT, LEFT = 0, 1
LATE, EARLY = 0, 1
EPS = 1e-06
CODE = 2.0**13
TINY = 2.0**-126


def encode(x):
    a = x * CODE
    a2 = a * a
    return (a2 * a2 * a).astype(BF16)


def decode(y):
    y = y.astype(F32)
    root = jnp.exp(jnp.log(jnp.maximum(jnp.abs(y), TINY)) * 0.2) * (1.0 / CODE)
    return jnp.where(y < 0, -root, root)


def nt(a, b):
    return lax.dot_general(a, b, (((1,), (1,)), ((), ())), preferred_element_type=F32)


def tn(a, b):
    return lax.dot_general(a, b, (((0,), (0,)), ((), ())), preferred_element_type=F32)


def kernel(
    img_hbm,
    txt_hbm,
    both_ref,
    loss_ref,
    gi_ref,
    gt_ref,
    img_ref,
    txt_ref,
    img,
    txt,
    part,
    coefs,
    sums,
    rs_send,
    rs_recv,
    core_recv,
    y_send,
    y_recv,
    unit_i,
    unit_t,
    inv_i,
    inv_t,
    loss_part,
    loss_send,
    loss_recv,
    in_sem,
    ag_ssem,
    ag_rsem,
    rs_ssem,
    rs_rsem,
    loss_ssem,
    loss_rsem,
    t_ssem,
    t_rsem,
    c_ssem,
    c_rsem,
    y_ssem,
    y_rsem,
):
    rows = img_ref.shape[0]
    half = rows // 2
    sub = half // 2
    me = lax.axis_index("blk")
    n = RING * QUAD
    to = (lax.rem(me + QUAD, n), lax.rem(me + n - QUAD, n))
    other_core = me + 1 - 2 * lax.rem(me, 2)
    other_y = me + 2 - 4 * lax.rem(lax.div(me, 2), 2)

    def copy(src, dst, ssem, rsem, device):
        return pltpu.make_async_remote_copy(
            src_ref=src,
            dst_ref=dst,
            send_sem=ssem,
            recv_sem=rsem,
            device_id={"blk": device},
            device_id_type=MESH,
        )

    barrier = pltpu.get_barrier_semaphore()
    for peer in (*to, other_core, other_y):
        pl.semaphore_signal(barrier, inc=1, device_id={"blk": peer}, device_id_type=MESH)

    def load(i):
        src, dst = ((img_hbm, img_ref), (txt_hbm, txt_ref))[i // 2]
        some = pl.ds(i % 2 * half, half)
        return pltpu.make_async_copy(src.at[some, :], dst.at[some, :], in_sem.at[i])

    for i in range(4):
        load(i).start()

    def normalize(src, at, size, unit, inv, out):
        values = src[pl.ds(at, size), :].astype(F32)
        norm = jnp.sqrt(jnp.sum(values * values, axis=1, keepdims=True) + EPS)
        inverse = 1.0 / norm
        u = values * inverse
        unit[pl.ds(at, size), :] = u
        inv[pl.ds(at, size), :] = jnp.broadcast_to(inverse, (size, 128))
        out[pl.ds(at, size), :] = u.astype(BF16)

    def place(way, i, s):
        side = way if i < 6 else 1 - way
        return s * half + side * sub

    def gather(way, i, s):
        if i < 2:
            piece = i if way == RIGHT else 1 - i
            src = img.at[0, pl.ds(piece * half + s * sub, sub), :]
        else:
            src = img.at[i - 1, pl.ds(place(way, i - 2, s), sub), :]
        dst = img.at[i + 1, pl.ds(place(way, i, s), sub), :]
        return copy(src, dst, ag_ssem.at[way, i, s], ag_rsem.at[way, i, s], to[way])

    for i in range(2):
        load(i).wait()
        normalize(img_ref, i * half, half, unit_i, inv_i, img.at[0])
        if i == 0:
            pl.semaphore_wait(barrier, 4)
        for s in range(2):
            gather(i, 0, s).start()
    for s in range(2):
        for way in (RIGHT, LEFT):
            gather(way, 1, s).start()

    for i in range(2):
        load(2 + i).wait()
        normalize(txt_ref, i * half, half, unit_t, inv_t, txt)

    scale = both_ref[0:1, 0:1]
    bias = both_ref[1:2, 0:1]

    def text_copy(i):
        src = (0, 0, 2)[i]
        dst = (1, 2, 3)[i]
        device = (other_core, other_y, other_core)[i]
        return copy(
            txt.at[pl.ds(src * rows, rows), :],
            txt.at[pl.ds(dst * rows, rows), :],
            t_ssem.at[i],
            t_rsem.at[i],
            device,
        )

    text_copy(1).start()
    text_copy(0).start()

    def tile(block, at, size, maybe_own=False):
        some = pl.ds(at, size)
        wide = 2 * rows
        total = jnp.zeros((size, rows), F32)
        for h in range(2):
            m = nt(img[block, some, :], txt[pl.ds(h * wide, wide), :]) * scale + bias
            if maybe_own and h == 0:
                row = lax.broadcasted_iota(jnp.int32, m.shape, 0)
                col = lax.broadcasted_iota(jnp.int32, m.shape, 1)
                eye = row + jnp.where(block == 0, 0, 2 * wide) == col
                m = jnp.where(eye, -m, m)
            e = jnp.exp(-jnp.abs(m))
            soft = jnp.maximum(m, 0.0) + jnp.log1p(e)
            r = 1.0 / (1.0 + e)
            coef = jnp.where(m >= 0, r, e * r)
            if maybe_own and h == 0:
                coef = jnp.where(eye, -coef, coef)
            total = total + soft[:, :rows] + soft[:, rows:]
            coefs[block, some, pl.ds(h * wide, wide)] = coef.astype(BF16)
        part[block, some, :] = jnp.dot(
            coefs[block, some, :], txt[...], preferred_element_type=F32
        )
        if size < rows:
            total = jnp.concatenate([total, total], axis=0)
        across = jnp.sum(total.T, axis=0, keepdims=True)
        if size < rows:
            lane = lax.broadcasted_iota(jnp.int32, (1, rows), 1)
            across = jnp.where(lane < at, loss_part[block], across)
        loss_part[block] = across

    def serve(i, s):
        for way in (RIGHT, LEFT):
            gather(way, i, s).wait_recv()
            if i < 5:
                gather(way, i + 2, s).start()

    def gather_wait(way, i, s):
        row = pl.multiple_of(place(way, i, s), sub)
        some = img.at[i + 1, pl.ds(row, sub), :]
        copy(some, some, ag_ssem.at[way, i, s], ag_rsem.at[way, i, s], to[way]).wait_recv()

    def block_of(kind, j):
        return (7, 6, 4, 2)[j] if kind == LATE else (5, 3, 1)[j]

    def chunk(way, kind, j, s):
        at = 4 * kind + j
        some = pl.ds(pl.multiple_of(s * sub, sub), sub)
        return copy(
            rs_send.at[way, at, some, :],
            rs_recv.at[way, at, some, :],
            rs_ssem.at[way, at, s],
            rs_rsem.at[way, at, s],
            to[way],
        )

    def pass_on(kind, j, first=0, count=2):
        def one(s, _):
            some = pl.ds(pl.multiple_of(s * sub, sub), sub)
            for way in (RIGHT, LEFT):
                row = pl.multiple_of(s * half + (1 - way) * sub, sub)
                x = part[block_of(kind, j), pl.ds(row, sub), :]
                if j > 0:
                    chunk(way, kind, j - 1, s).wait_recv()
                    x = x + decode(rs_recv[way, 4 * kind + j - 1, some, :])
                rs_send[way, 4 * kind + j, some, :] = encode(x)
                chunk(way, kind, j, s).start()
            return 0

        lax.fori_loop(first, first + count, one, 0)

    def loss_copy(way, kind, j):
        at = 4 * kind + j
        return copy(
            loss_send.at[way, at],
            loss_recv.at[way, at],
            loss_ssem.at[way, at],
            loss_rsem.at[way, at],
            to[way],
        )

    def loss_on(kind, j):
        for way in (RIGHT, LEFT):
            x = loss_part[block_of(kind, j)]
            if j > 0:
                loss_copy(way, kind, j - 1).wait_recv()
                x = x + loss_recv[way, 4 * kind + j - 1]
            loss_send[way, 4 * kind + j] = x
            loss_copy(way, kind, j).start()

    for i in range(2):
        serve(i, 0)
        serve(i, 1)
    text_copy(1).wait_recv()
    text_copy(2).start()
    serve(2, 0)
    serve(2, 1)
    text_copy(0).wait_recv()
    text_copy(2).wait_recv()

    def work(k, _):
        @pl.when(k == 1)
        def _():
            serve(3, 0)

        @pl.when(k == 2)
        def _():
            serve(3, 1)

        @pl.when(k == 4)
        def _():
            serve(4, 0)
            serve(4, 1)

        @pl.when(k == 5)
        def _():
            loss_on(EARLY, 0)
            pass_on(EARLY, 0)

        @pl.when(k == 6)
        def _():
            serve(5, 0)
            serve(5, 1)

        tile(jnp.where(k < 5, k + 1, jnp.where(k == 5, 0, 6)), 0, rows, True)
        return 0

    lax.fori_loop(0, 7, work, 0)

    def farthest(s, _):
        for way in (RIGHT, LEFT):
            gather_wait(way, 6, s)
        tile(7, pl.multiple_of(s * half, half), half)
        pl.when(s == 1)(lambda: loss_on(LATE, 0))
        pass_on(LATE, 0, s, 1)
        return 0

    lax.fori_loop(0, 2, farthest, 0)

    def text_sums(b):
        sums[b] = tn(
            coefs[:, :, pl.ds(pl.multiple_of(b * rows, rows), rows)].reshape(RING * rows, rows),
            img[...].reshape(RING * rows, img.shape[2]),
        )

    def core_copy(i):
        return copy(sums.at[1 + 2 * i], core_recv.at[i], c_ssem.at[i], c_rsem.at[i], other_core)

    y_copy = copy(y_send, y_recv, y_ssem.at[0], y_rsem.at[0], other_y)

    def sums_work(k, _):
        b = jnp.where(k == 0, 3, jnp.where(k == 1, 1, jnp.where(k == 2, 2, 0)))
        text_sums(b)

        @pl.when(k == 0)
        def _():
            core_copy(1).start()

        @pl.when(k == 1)
        def _():
            core_copy(0).start()
            loss_on(EARLY, 1)
            pass_on(EARLY, 1)

        return 0

    lax.fori_loop(0, QUAD, sums_work, 0)
    loss_on(LATE, 1)
    pass_on(LATE, 1)
    core_copy(1).wait_recv()
    y_send[...] = encode(sums[2] + core_recv[1])
    y_copy.start()
    loss_on(EARLY, 2)
    pass_on(EARLY, 2, 0, 1)
    loss_on(LATE, 2)
    pass_on(LATE, 2)
    pass_on(EARLY, 2, 1, 1)
    core_copy(0).wait_recv()
    sums[0] += core_recv[0]
    loss_on(LATE, 3)
    pass_on(LATE, 3)

    def sent(i, _):
        for way in (RIGHT, LEFT):
            for s in range(2):
                some = img.at[i, pl.ds(s * sub, sub), :]
                copy(some, some, ag_ssem.at[way, i, s], ag_rsem.at[way, i, s], to[way]).wait_send()
        return 0

    lax.fori_loop(0, 7, sent, 0)
    for i in range(3):
        text_copy(i).wait_send()
    for i in range(2):
        core_copy(i).wait_send()

    def summed(at):
        for way in (RIGHT, LEFT):
            for s in range(2):
                some = rs_send.at[way, at, pl.ds(s * sub, sub), :]
                copy(some, some, rs_ssem.at[way, at, s], rs_rsem.at[way, at, s], to[way]).wait_send()
            x = loss_send.at[way, at]
            copy(x, x, loss_ssem.at[way, at], loss_rsem.at[way, at], to[way]).wait_send()

    lax.fori_loop(0, 3, lambda i, _: (summed(i), 0)[1], 0)
    lax.fori_loop(4, 7, lambda i, _: (summed(i), 0)[1], 0)

    def unnormal(g, u, inv):
        along = jnp.sum(u * g, axis=1, keepdims=True)
        return (g - u * along) * (inv[:, 0:1] * scale)

    def last(way, kind, s):
        some = pl.ds(pl.multiple_of(s * sub, sub), sub)
        chunk(way, kind, 3 - kind, s).wait_recv()
        at = (half if (way == RIGHT) == (kind == EARLY) else 0) + s * sub
        at = pl.ds(pl.multiple_of(at, sub), sub)
        return at, part[0, at, :] + decode(rs_recv[way, 4 * kind + 3 - kind, some, :])

    def add_early(s, _):
        for way in (RIGHT, LEFT):
            at, x = last(way, EARLY, s)
            part[0, at, :] = x
        return 0

    lax.fori_loop(0, 2, add_early, 0)
    y_copy.wait_recv()

    def finish_text(i, _):
        at = pl.ds(pl.multiple_of(i * sub, sub), sub)
        g = sums[0, at, :] + decode(y_recv[at, :])
        gt_ref[at, :] = unnormal(g, unit_t[at, :], inv_t[at, :])
        return 0

    lax.fori_loop(0, 4, finish_text, 0)

    def lanes(way, kind):
        loss_copy(way, kind, 3 - kind).wait_recv()
        x = loss_recv[way, 4 * kind + 3 - kind]
        at = (1 - way) * sub
        return [x[:, s * half + at : s * half + at + sub] for s in range(2)]

    loss_ref[...] = (
        loss_part[0]
        + jnp.concatenate(lanes(RIGHT, LATE) + lanes(RIGHT, EARLY), axis=1)
        + jnp.concatenate(lanes(LEFT, EARLY) + lanes(LEFT, LATE), axis=1)
    )
    y_copy.wait_send()

    def finish(s, _):
        for way in (RIGHT, LEFT):
            at, g = last(way, LATE, s)
            gi_ref[at, :] = unnormal(g, unit_i[at, :], inv_i[at, :])
        return 0

    lax.fori_loop(0, 2, finish, 0)
    summed(3)


def write_out(loss_in, gi_in, gt_in, loss_out, gi_out, gt_out, row, sem):
    copies = [
        pltpu.make_async_copy(gi_in, gi_out, sem.at[0]),
        pltpu.make_async_copy(gt_in, gt_out, sem.at[1]),
        pltpu.make_async_copy(row, loss_out, sem.at[2]),
    ]
    row[...] = loss_in[0]
    for c in copies:
        c.start()
    for c in copies:
        c.wait()


def per_device(image_embed, text_embed, logit_scale, logit_bias):
    rows, width = image_embed.shape
    half = rows // 2
    dma = pltpu.SemaphoreType.DMA
    vmem = pl.BlockSpec(memory_space=pltpu.VMEM)
    hbm = pl.BlockSpec(memory_space=pltpu.HBM)
    image_embed = pltpu.with_memory_space_constraint(image_embed, pltpu.HBM)
    text_embed = pltpu.with_memory_space_constraint(text_embed, pltpu.HBM)
    row = lax.broadcasted_iota(jnp.int32, (8, 128), 0)
    both = jnp.where(row == 0, logit_scale[0], logit_bias[0])
    anywhere = pl.BlockSpec(memory_space=pl.ANY)
    results = pl.pallas_call(
        kernel,
        out_shape=(
            pltpu.VMEM((1, rows), F32),
            pltpu.VMEM((rows, width), F32),
            pltpu.VMEM((rows, width), F32),
        ),
        in_specs=[hbm, hbm, vmem],
        out_specs=(vmem, vmem, vmem),
        scratch_shapes=[
            pltpu.VMEM((rows, width), BF16),
            pltpu.VMEM((rows, width), BF16),
            pltpu.VMEM((RING, rows, width), BF16),
            pltpu.VMEM((QUAD * rows, width), BF16),
            pltpu.VMEM((RING, rows, width), F32),
            pltpu.VMEM((RING, rows, QUAD * rows), BF16),
            pltpu.VMEM((QUAD, rows, width), F32),
            pltpu.VMEM((2, 7, half, width), BF16),
            pltpu.VMEM((2, 7, half, width), BF16),
            pltpu.VMEM((2, rows, width), F32),
            pltpu.VMEM((rows, width), BF16),
            pltpu.VMEM((rows, width), BF16),
            pltpu.VMEM((rows, width), F32),
            pltpu.VMEM((rows, width), F32),
            pltpu.VMEM((rows, 128), F32),
            pltpu.VMEM((rows, 128), F32),
            pltpu.VMEM((RING, 1, rows), F32),
            pltpu.VMEM((2, 7, 1, rows), F32),
            pltpu.VMEM((2, 7, 1, rows), F32),
            dma((4,)),
            dma((2, 7, 2)),
            dma((2, 7, 2)),
            dma((2, 7, 2)),
            dma((2, 7, 2)),
            dma((2, 7)),
            dma((2, 7)),
            dma((3,)),
            dma((3,)),
            dma((2,)),
            dma((2,)),
            dma((1,)),
            dma((1,)),
        ],
        compiler_params=pltpu.CompilerParams(
            collective_id=0, has_side_effects=True, vmem_limit_bytes=48 * 2**20
        ),
        cost_estimate=pl.CostEstimate(
            flops=3 * 2 * 1024 * 512 * width, bytes_accessed=6 * rows * width, transcendentals=0
        ),
    )(image_embed, text_embed, both)
    return pl.pallas_call(
        write_out,
        out_shape=(
            jax.ShapeDtypeStruct((rows,), F32),
            jax.ShapeDtypeStruct((rows, width), F32),
            jax.ShapeDtypeStruct((rows, width), F32),
        ),
        in_specs=[vmem, vmem, vmem],
        out_specs=(anywhere, anywhere, anywhere),
        scratch_shapes=[pltpu.VMEM((rows,), F32), dma((3,))],
        compiler_params=pltpu.CompilerParams(vmem_limit_bytes=2**20),
        cost_estimate=pl.CostEstimate(flops=0, bytes_accessed=16 * rows * width, transcendentals=0),
    )(*results)


def solution(mesh):
    placed = (P(("group", "blk"), None), P(("group", "blk"), None), P(), P())
    return jax.shard_map(
        per_device,
        mesh=mesh,
        in_specs=placed,
        out_specs=(P(("group", "blk")), P(("group", "blk"), None), P(("group", "blk"), None)),
        check_vma=False,
    )
```

```python
import functools

import jax
import jax.numpy as jnp
from jax import lax
from jax.experimental import pallas as pl
from jax.experimental.pallas import tpu as pltpu
from jax.sharding import PartitionSpec as P

MESH = pl.DeviceIdType.MESH
F32 = jnp.float32
BF16 = jnp.bfloat16

RING = 8
QUAD = 4
RIGHT, LEFT = 0, 1
LATE, EARLY = 0, 1
EPS = 1e-06
CODE = 2.0**13
TINY = 2.0**-126


def encode(x):
    a = x * CODE
    a2 = a * a
    return (a2 * a2 * a).astype(BF16)


def decode(y):
    y = y.astype(F32)
    root = jnp.exp(jnp.log(jnp.maximum(jnp.abs(y), TINY)) * 0.2) * (1.0 / CODE)
    return jnp.where(y < 0, -root, root)


def nt(a, b):
    return lax.dot_general(a, b, (((1,), (1,)), ((), ())), preferred_element_type=F32)


def tn(a, b):
    return lax.dot_general(a, b, (((0,), (0,)), ((), ())), preferred_element_type=F32)


def unnormal(g, u, inv, scale):
    along = jnp.sum(u * g, axis=1, keepdims=True)
    return (g - u * along) * (inv[:, 0:1] * scale)


def kernel(
    img_hbm,
    txt_hbm,
    both_ref,
    loss_ref,
    gi_ref,
    gt_ref,
    late_ref,
    unit_i,
    inv_i,
    img_ref,
    txt_ref,
    img,
    txt,
    part,
    coefs,
    sums,
    rs_send,
    rs_recv,
    core_recv,
    y_send,
    y_recv,
    unit_t,
    inv_t,
    loss_part,
    loss_send,
    loss_recv,
    in_sem,
    ag_ssem,
    ag_rsem,
    rs_ssem,
    rs_rsem,
    loss_ssem,
    loss_rsem,
    t_ssem,
    t_rsem,
    c_ssem,
    c_rsem,
    y_ssem,
    y_rsem,
):
    rows = img_ref.shape[0]
    half = rows // 2
    sub = half // 2
    me = lax.axis_index("blk")
    n = RING * QUAD
    to = (lax.rem(me + QUAD, n), lax.rem(me + n - QUAD, n))
    other_core = me + 1 - 2 * lax.rem(me, 2)
    other_y = me + 2 - 4 * lax.rem(lax.div(me, 2), 2)

    def copy(src, dst, ssem, rsem, device):
        return pltpu.make_async_remote_copy(
            src_ref=src,
            dst_ref=dst,
            send_sem=ssem,
            recv_sem=rsem,
            device_id={"blk": device},
            device_id_type=MESH,
        )

    barrier = pltpu.get_barrier_semaphore()
    for peer in (*to, other_core, other_y):
        pl.semaphore_signal(barrier, inc=1, device_id={"blk": peer}, device_id_type=MESH)

    def load(i):
        src, dst = ((img_hbm, img_ref), (txt_hbm, txt_ref))[i // 2]
        some = pl.ds(i % 2 * half, half)
        return pltpu.make_async_copy(src.at[some, :], dst.at[some, :], in_sem.at[i])

    for i in range(4):
        load(i).start()

    def normalize(src, at, size, unit, inv, out):
        values = src[pl.ds(at, size), :].astype(F32)
        norm = jnp.sqrt(jnp.sum(values * values, axis=1, keepdims=True) + EPS)
        inverse = 1.0 / norm
        u = values * inverse
        unit[pl.ds(at, size), :] = u
        inv[pl.ds(at, size), :] = jnp.broadcast_to(inverse, (size, 128))
        out[pl.ds(at, size), :] = u.astype(BF16)

    def place(way, i, s):
        side = way if i < 6 else 1 - way
        return s * half + side * sub

    def gather(way, i, s):
        if i < 2:
            piece = i if way == RIGHT else 1 - i
            src = img.at[0, pl.ds(piece * half + s * sub, sub), :]
        else:
            src = img.at[i - 1, pl.ds(place(way, i - 2, s), sub), :]
        dst = img.at[i + 1, pl.ds(place(way, i, s), sub), :]
        return copy(src, dst, ag_ssem.at[way, i, s], ag_rsem.at[way, i, s], to[way])

    for i in range(2):
        load(i).wait()
        normalize(img_ref, i * half, half, unit_i, inv_i, img.at[0])
        if i == 0:
            pl.semaphore_wait(barrier, 4)
        for s in range(2):
            gather(i, 0, s).start()
    for s in range(2):
        for way in (RIGHT, LEFT):
            gather(way, 1, s).start()

    for i in range(2):
        load(2 + i).wait()
        normalize(txt_ref, i * half, half, unit_t, inv_t, txt)

    scale = both_ref[0:1, 0:1]
    bias = both_ref[1:2, 0:1]

    def text_copy(i):
        src = (0, 0, 2)[i]
        dst = (1, 2, 3)[i]
        device = (other_core, other_y, other_core)[i]
        return copy(
            txt.at[pl.ds(src * rows, rows), :],
            txt.at[pl.ds(dst * rows, rows), :],
            t_ssem.at[i],
            t_rsem.at[i],
            device,
        )

    text_copy(1).start()
    text_copy(0).start()

    def tile(block, at, size, maybe_own=False):
        some = pl.ds(at, size)
        wide = 2 * rows
        total = jnp.zeros((size, rows), F32)
        for h in range(2):
            m = nt(img[block, some, :], txt[pl.ds(h * wide, wide), :]) * scale + bias
            if maybe_own and h == 0:
                row = lax.broadcasted_iota(jnp.int32, m.shape, 0)
                col = lax.broadcasted_iota(jnp.int32, m.shape, 1)
                eye = row + jnp.where(block == 0, 0, 2 * wide) == col
                m = jnp.where(eye, -m, m)
            e = jnp.exp(-jnp.abs(m))
            soft = jnp.maximum(m, 0.0) + jnp.log1p(e)
            r = 1.0 / (1.0 + e)
            coef = jnp.where(m >= 0, r, e * r)
            if maybe_own and h == 0:
                coef = jnp.where(eye, -coef, coef)
            total = total + soft[:, :rows] + soft[:, rows:]
            coefs[block, some, pl.ds(h * wide, wide)] = coef.astype(BF16)
        part[block, some, :] = jnp.dot(
            coefs[block, some, :], txt[...], preferred_element_type=F32
        )
        if size < rows:
            total = jnp.concatenate([total, total], axis=0)
        across = jnp.sum(total.T, axis=0, keepdims=True)
        if size < rows:
            lane = lax.broadcasted_iota(jnp.int32, (1, rows), 1)
            across = jnp.where(lane < at, loss_part[block], across)
        loss_part[block] = across

    def serve(i, s):
        for way in (RIGHT, LEFT):
            gather(way, i, s).wait_recv()
            if i < 5:
                gather(way, i + 2, s).start()

    def gather_wait(way, i, s):
        row = pl.multiple_of(place(way, i, s), sub)
        some = img.at[i + 1, pl.ds(row, sub), :]
        copy(some, some, ag_ssem.at[way, i, s], ag_rsem.at[way, i, s], to[way]).wait_recv()

    def block_of(kind, j):
        return (7, 6, 4, 2)[j] if kind == LATE else (5, 3, 1)[j]

    def chunk(way, kind, j, s):
        at = 4 * kind + j
        some = pl.ds(pl.multiple_of(s * sub, sub), sub)
        very_last = kind == LATE and j == 3 and s == 1
        return copy(
            rs_send.at[way, at, some, :],
            late_ref.at[way] if very_last else rs_recv.at[way, at, some, :],
            rs_ssem.at[way, at, s],
            rs_rsem.at[way, at, s],
            to[way],
        )

    def pass_on(kind, j, first=0, count=2):
        def one(s, _):
            some = pl.ds(pl.multiple_of(s * sub, sub), sub)
            for way in (RIGHT, LEFT):
                row = pl.multiple_of(s * half + (1 - way) * sub, sub)
                x = part[block_of(kind, j), pl.ds(row, sub), :]
                if j > 0:
                    chunk(way, kind, j - 1, s).wait_recv()
                    x = x + decode(rs_recv[way, 4 * kind + j - 1, some, :])
                rs_send[way, 4 * kind + j, some, :] = encode(x)
                chunk(way, kind, j, s).start()
            return 0

        if j == 3:
            one(0, 0)
            one(1, 0)
        else:
            lax.fori_loop(first, first + count, one, 0)

    def loss_copy(way, kind, j):
        at = 4 * kind + j
        return copy(
            loss_send.at[way, at],
            loss_recv.at[way, at],
            loss_ssem.at[way, at],
            loss_rsem.at[way, at],
            to[way],
        )

    def loss_on(kind, j):
        for way in (RIGHT, LEFT):
            x = loss_part[block_of(kind, j)]
            if j > 0:
                loss_copy(way, kind, j - 1).wait_recv()
                x = x + loss_recv[way, 4 * kind + j - 1]
            loss_send[way, 4 * kind + j] = x
            loss_copy(way, kind, j).start()

    for i in range(2):
        serve(i, 0)
        serve(i, 1)
    text_copy(1).wait_recv()
    text_copy(2).start()
    serve(2, 0)
    serve(2, 1)
    text_copy(0).wait_recv()
    text_copy(2).wait_recv()

    def work(k, _):
        @pl.when(k == 1)
        def _():
            serve(3, 0)

        @pl.when(k == 2)
        def _():
            serve(3, 1)

        @pl.when(k == 4)
        def _():
            serve(4, 0)
            serve(4, 1)

        @pl.when(k == 5)
        def _():
            loss_on(EARLY, 0)
            pass_on(EARLY, 0)

        @pl.when(k == 6)
        def _():
            serve(5, 0)
            serve(5, 1)

        tile(jnp.where(k < 5, k + 1, jnp.where(k == 5, 0, 6)), 0, rows, True)
        return 0

    lax.fori_loop(0, 7, work, 0)

    def farthest(s, _):
        for way in (RIGHT, LEFT):
            gather_wait(way, 6, s)
        tile(7, pl.multiple_of(s * half, half), half)
        pl.when(s == 1)(lambda: loss_on(LATE, 0))
        pass_on(LATE, 0, s, 1)
        return 0

    lax.fori_loop(0, 2, farthest, 0)

    def text_sums(b):
        sums[b] = tn(
            coefs[:, :, pl.ds(pl.multiple_of(b * rows, rows), rows)].reshape(RING * rows, rows),
            img[...].reshape(RING * rows, img.shape[2]),
        )

    def core_copy(i):
        return copy(sums.at[1 + 2 * i], core_recv.at[i], c_ssem.at[i], c_rsem.at[i], other_core)

    y_copy = copy(y_send, y_recv, y_ssem.at[0], y_rsem.at[0], other_y)

    def sums_work(k, _):
        b = jnp.where(k == 0, 3, jnp.where(k == 1, 1, jnp.where(k == 2, 2, 0)))
        text_sums(b)

        @pl.when(k == 0)
        def _():
            core_copy(1).start()

        @pl.when(k == 1)
        def _():
            core_copy(0).start()
            loss_on(EARLY, 1)
            pass_on(EARLY, 1)

        return 0

    lax.fori_loop(0, QUAD, sums_work, 0)
    loss_on(LATE, 1)
    pass_on(LATE, 1)
    core_copy(1).wait_recv()
    y_send[...] = encode(sums[2] + core_recv[1])
    y_copy.start()
    loss_on(EARLY, 2)
    pass_on(EARLY, 2, 0, 1)
    loss_on(LATE, 2)
    pass_on(LATE, 2)
    pass_on(EARLY, 2, 1, 1)
    core_copy(0).wait_recv()
    sums[0] += core_recv[0]
    loss_on(LATE, 3)
    pass_on(LATE, 3)

    def sent(i, _):
        for way in (RIGHT, LEFT):
            for s in range(2):
                some = img.at[i, pl.ds(s * sub, sub), :]
                copy(some, some, ag_ssem.at[way, i, s], ag_rsem.at[way, i, s], to[way]).wait_send()
        return 0

    lax.fori_loop(0, 7, sent, 0)
    for i in range(3):
        text_copy(i).wait_send()
    for i in range(2):
        core_copy(i).wait_send()

    def summed(at):
        for way in (RIGHT, LEFT):
            for s in range(2):
                some = rs_send.at[way, at, pl.ds(s * sub, sub), :]
                copy(some, some, rs_ssem.at[way, at, s], rs_rsem.at[way, at, s], to[way]).wait_send()
            x = loss_send.at[way, at]
            copy(x, x, loss_ssem.at[way, at], loss_rsem.at[way, at], to[way]).wait_send()

    lax.fori_loop(0, 3, lambda i, _: (summed(i), 0)[1], 0)
    lax.fori_loop(4, 7, lambda i, _: (summed(i), 0)[1], 0)

    def own_rows(way, kind, s):
        at = (half if (way == RIGHT) == (kind == EARLY) else 0) + s * sub
        return pl.ds(pl.multiple_of(at, sub), sub)

    def last(way, kind, s):
        some = pl.ds(pl.multiple_of(s * sub, sub), sub)
        chunk(way, kind, 3 - kind, s).wait_recv()
        at = own_rows(way, kind, s)
        return at, part[0, at, :] + decode(rs_recv[way, 4 * kind + 3 - kind, some, :])

    def add_early(s, _):
        for way in (RIGHT, LEFT):
            at, x = last(way, EARLY, s)
            part[0, at, :] = x
        return 0

    lax.fori_loop(0, 2, add_early, 0)
    y_copy.wait_recv()

    def finish_text(i, _):
        at = pl.ds(pl.multiple_of(i * sub, sub), sub)
        g = sums[0, at, :] + decode(y_recv[at, :])
        gt_ref[at, :] = unnormal(g, unit_t[at, :], inv_t[at, :], scale)
        return 0

    lax.fori_loop(0, 4, finish_text, 0)

    def lanes(way, kind):
        loss_copy(way, kind, 3 - kind).wait_recv()
        x = loss_recv[way, 4 * kind + 3 - kind]
        at = (1 - way) * sub
        return [x[:, s * half + at : s * half + at + sub] for s in range(2)]

    loss_ref[...] = (
        loss_part[0]
        + jnp.concatenate(lanes(RIGHT, LATE) + lanes(RIGHT, EARLY), axis=1)
        + jnp.concatenate(lanes(LEFT, EARLY) + lanes(LEFT, LATE), axis=1)
    )
    y_copy.wait_send()

    for way in (RIGHT, LEFT):
        at = own_rows(way, LATE, 1)
        gi_ref[at, :] = part[0, at, :]
    for way in (RIGHT, LEFT):
        at, g = last(way, LATE, 0)
        gi_ref[at, :] = unnormal(g, unit_i[at, :], inv_i[at, :], scale)
    for way in (RIGHT, LEFT):
        chunk(way, LATE, 3, 1).wait_recv()
    summed(3)


def write_out(
    loss_in, gi_in, gt_in, late, unit, inv, both, loss_out, gi_out, gt_out, row, rest, sem
):
    sub = late.shape[1]
    row[...] = loss_in[0]
    copies = [
        pltpu.make_async_copy(gt_in, gt_out, sem.at[0]),
        pltpu.make_async_copy(row, loss_out, sem.at[1]),
    ]
    for way in (RIGHT, LEFT):
        some = pl.ds(way * 2 * sub, sub)
        copies.append(pltpu.make_async_copy(gi_in.at[some, :], gi_out.at[some, :], sem.at[2 + way]))
    for c in copies:
        c.start()
    scale = both[0:1, 0:1]
    for way in (RIGHT, LEFT):
        some = pl.ds(way * 2 * sub + sub, sub)
        g = gi_in[some, :] + decode(late[way])
        rest[way] = unnormal(g, unit[some, :], inv[some, :], scale)
        c = pltpu.make_async_copy(rest.at[way], gi_out.at[some, :], sem.at[4 + way])
        c.start()
        copies.append(c)
    for c in copies:
        c.wait()


def per_device(image_embed, text_embed, logit_scale, logit_bias):
    rows, width = image_embed.shape
    half = rows // 2
    dma = pltpu.SemaphoreType.DMA
    vmem = pl.BlockSpec(memory_space=pltpu.VMEM)
    hbm = pl.BlockSpec(memory_space=pltpu.HBM)
    image_embed = pltpu.with_memory_space_constraint(image_embed, pltpu.HBM)
    text_embed = pltpu.with_memory_space_constraint(text_embed, pltpu.HBM)
    row = lax.broadcasted_iota(jnp.int32, (8, 128), 0)
    both = jnp.where(row == 0, logit_scale[0], logit_bias[0])
    anywhere = pl.BlockSpec(memory_space=pl.ANY)
    results = pl.pallas_call(
        kernel,
        out_shape=(
            pltpu.VMEM((1, rows), F32),
            pltpu.VMEM((rows, width), F32),
            pltpu.VMEM((rows, width), F32),
            pltpu.VMEM((2, rows // 4, width), BF16),
            pltpu.VMEM((rows, width), F32),
            pltpu.VMEM((rows, 128), F32),
        ),
        in_specs=[hbm, hbm, vmem],
        out_specs=(vmem,) * 6,
        scratch_shapes=[
            pltpu.VMEM((rows, width), BF16),
            pltpu.VMEM((rows, width), BF16),
            pltpu.VMEM((RING, rows, width), BF16),
            pltpu.VMEM((QUAD * rows, width), BF16),
            pltpu.VMEM((RING, rows, width), F32),
            pltpu.VMEM((RING, rows, QUAD * rows), BF16),
            pltpu.VMEM((QUAD, rows, width), F32),
            pltpu.VMEM((2, 7, half, width), BF16),
            pltpu.VMEM((2, 7, half, width), BF16),
            pltpu.VMEM((2, rows, width), F32),
            pltpu.VMEM((rows, width), BF16),
            pltpu.VMEM((rows, width), BF16),
            pltpu.VMEM((rows, width), F32),
            pltpu.VMEM((rows, 128), F32),
            pltpu.VMEM((RING, 1, rows), F32),
            pltpu.VMEM((2, 7, 1, rows), F32),
            pltpu.VMEM((2, 7, 1, rows), F32),
            dma((4,)),
            dma((2, 7, 2)),
            dma((2, 7, 2)),
            dma((2, 7, 2)),
            dma((2, 7, 2)),
            dma((2, 7)),
            dma((2, 7)),
            dma((3,)),
            dma((3,)),
            dma((2,)),
            dma((2,)),
            dma((1,)),
            dma((1,)),
        ],
        compiler_params=pltpu.CompilerParams(
            collective_id=0, has_side_effects=True, vmem_limit_bytes=48 * 2**20
        ),
        cost_estimate=pl.CostEstimate(
            flops=3 * 2 * 1024 * 512 * width, bytes_accessed=6 * rows * width, transcendentals=0
        ),
    )(image_embed, text_embed, both)
    return pl.pallas_call(
        write_out,
        out_shape=(
            jax.ShapeDtypeStruct((rows,), F32),
            jax.ShapeDtypeStruct((rows, width), F32),
            jax.ShapeDtypeStruct((rows, width), F32),
        ),
        in_specs=[vmem] * 7,
        out_specs=(anywhere, anywhere, anywhere),
        scratch_shapes=[pltpu.VMEM((rows,), F32), pltpu.VMEM((2, rows // 4, width), F32), dma((6,))],
        compiler_params=pltpu.CompilerParams(vmem_limit_bytes=4 * 2**20),
        cost_estimate=pl.CostEstimate(flops=0, bytes_accessed=16 * rows * width, transcendentals=0),
    )(*results, both)


def solution(mesh):
    placed = (P(("group", "blk"), None), P(("group", "blk"), None), P(), P())
    return jax.shard_map(
        per_device,
        mesh=mesh,
        in_specs=placed,
        out_specs=(P(("group", "blk")), P(("group", "blk"), None), P(("group", "blk"), None)),
        check_vma=False,
    )
```

```python
import functools

import jax
import jax.numpy as jnp
from jax import lax
from jax.experimental import pallas as pl
from jax.experimental.pallas import tpu as pltpu
from jax.sharding import PartitionSpec as P

MESH = pl.DeviceIdType.MESH
F32 = jnp.float32
BF16 = jnp.bfloat16

RING = 8
QUAD = 4
RIGHT, LEFT = 0, 1
LATE, EARLY = 0, 1
EPS = 1e-06
CODE = 2.0**13
TINY = 2.0**-126


def encode(x):
    a = x * CODE
    a2 = a * a
    return (a2 * a2 * a).astype(BF16)


def decode(y):
    y = y.astype(F32)
    root = jnp.exp(jnp.log(jnp.maximum(jnp.abs(y), TINY)) * 0.2) * (1.0 / CODE)
    return jnp.where(y < 0, -root, root)


def nt(a, b):
    return lax.dot_general(a, b, (((1,), (1,)), ((), ())), preferred_element_type=F32)


def tn(a, b):
    return lax.dot_general(a, b, (((0,), (0,)), ((), ())), preferred_element_type=F32)


def unnormal(g, u, inv, scale):
    along = jnp.sum(u * g, axis=1, keepdims=True)
    return (g - u * along) * (inv[:, 0:1] * scale)


def kernel(
    img_hbm,
    txt_hbm,
    both_ref,
    loss_ref,
    gi_ref,
    gt_ref,
    late_ref,
    unit_i,
    inv_i,
    img_ref,
    txt_ref,
    img,
    txt,
    part,
    coefs,
    sums,
    rs_send,
    rs_recv,
    core_recv,
    y_send,
    y_recv,
    unit_t,
    inv_t,
    loss_part,
    loss_send,
    loss_recv,
    in_sem,
    ag_ssem,
    ag_rsem,
    rs_ssem,
    rs_rsem,
    loss_ssem,
    loss_rsem,
    t_ssem,
    t_rsem,
    c_ssem,
    c_rsem,
    y_ssem,
    y_rsem,
):
    rows = img_ref.shape[0]
    half = rows // 2
    sub = half // 2
    me = lax.axis_index("blk")
    n = RING * QUAD
    to = (lax.rem(me + QUAD, n), lax.rem(me + n - QUAD, n))
    other_core = me + 1 - 2 * lax.rem(me, 2)
    other_y = me + 2 - 4 * lax.rem(lax.div(me, 2), 2)

    def copy(src, dst, ssem, rsem, device):
        return pltpu.make_async_remote_copy(
            src_ref=src,
            dst_ref=dst,
            send_sem=ssem,
            recv_sem=rsem,
            device_id={"blk": device},
            device_id_type=MESH,
        )

    barrier = pltpu.get_barrier_semaphore()
    for peer in (*to, other_core, other_y):
        pl.semaphore_signal(barrier, inc=1, device_id={"blk": peer}, device_id_type=MESH)

    def load(i):
        src, dst = ((img_hbm, img_ref), (txt_hbm, txt_ref))[i // 2]
        some = pl.ds(i % 2 * half, half)
        return pltpu.make_async_copy(src.at[some, :], dst.at[some, :], in_sem.at[i])

    for i in range(4):
        load(i).start()

    def normalize(src, at, size, unit, inv, out):
        values = src[pl.ds(at, size), :].astype(F32)
        norm = jnp.sqrt(jnp.sum(values * values, axis=1, keepdims=True) + EPS)
        inverse = 1.0 / norm
        u = values * inverse
        unit[pl.ds(at, size), :] = u
        inv[pl.ds(at, size), :] = jnp.broadcast_to(inverse, (size, 128))
        out[pl.ds(at, size), :] = u.astype(BF16)

    def place(way, i, s):
        side = way if i < 6 else 1 - way
        return s * half + side * sub

    def gather(way, i, s):
        if i < 2:
            piece = i if way == RIGHT else 1 - i
            src = img.at[0, pl.ds(piece * half + s * sub, sub), :]
        else:
            src = img.at[i - 1, pl.ds(place(way, i - 2, s), sub), :]
        dst = img.at[i + 1, pl.ds(place(way, i, s), sub), :]
        return copy(src, dst, ag_ssem.at[0], ag_rsem.at[way, i, s], to[way])

    for i in range(2):
        load(i).wait()
        normalize(img_ref, i * half, half, unit_i, inv_i, img.at[0])
        if i == 0:
            pl.semaphore_wait(barrier, 4)
        for s in range(2):
            gather(i, 0, s).start()
    for s in range(2):
        for way in (RIGHT, LEFT):
            gather(way, 1, s).start()

    for i in range(2):
        load(2 + i).wait()
        normalize(txt_ref, i * half, half, unit_t, inv_t, txt)

    scale = both_ref[0:1, 0:1]
    bias = both_ref[1:2, 0:1]

    def text_copy(i):
        src = (0, 0, 2)[i]
        dst = (1, 2, 3)[i]
        device = (other_core, other_y, other_core)[i]
        return copy(
            txt.at[pl.ds(src * rows, rows), :],
            txt.at[pl.ds(dst * rows, rows), :],
            t_ssem.at[i],
            t_rsem.at[i],
            device,
        )

    text_copy(1).start()
    text_copy(0).start()

    def tile(block, at, size, maybe_own=False):
        some = pl.ds(at, size)
        wide = 2 * rows
        total = jnp.zeros((size, rows), F32)
        for h in range(2):
            m = nt(img[block, some, :], txt[pl.ds(h * wide, wide), :]) * scale + bias
            if maybe_own and h == 0:
                row = lax.broadcasted_iota(jnp.int32, m.shape, 0)
                col = lax.broadcasted_iota(jnp.int32, m.shape, 1)
                eye = row + jnp.where(block == 0, 0, 2 * wide) == col
                m = jnp.where(eye, -m, m)
            e = jnp.exp(-jnp.abs(m))
            soft = jnp.maximum(m, 0.0) + jnp.log1p(e)
            r = 1.0 / (1.0 + e)
            coef = jnp.where(m >= 0, r, e * r)
            if maybe_own and h == 0:
                coef = jnp.where(eye, -coef, coef)
            total = total + soft[:, :rows] + soft[:, rows:]
            coefs[block, some, pl.ds(h * wide, wide)] = coef.astype(BF16)
        part[block, some, :] = jnp.dot(
            coefs[block, some, :], txt[...], preferred_element_type=F32
        )
        if size < rows:
            total = jnp.concatenate([total, total], axis=0)
        across = jnp.sum(total.T, axis=0, keepdims=True)
        if size < rows:
            lane = lax.broadcasted_iota(jnp.int32, (1, rows), 1)
            across = jnp.where(lane < at, loss_part[block], across)
        loss_part[block] = across

    def serve(i, s):
        for way in (RIGHT, LEFT):
            gather(way, i, s).wait_recv()
            if i < 5:
                gather(way, i + 2, s).start()

    def gather_wait(way, i, s):
        row = pl.multiple_of(place(way, i, s), sub)
        some = img.at[i + 1, pl.ds(row, sub), :]
        copy(some, some, ag_ssem.at[0], ag_rsem.at[way, i, s], to[way]).wait_recv()

    def block_of(kind, j):
        return (7, 6, 4, 2)[j] if kind == LATE else (5, 3, 1)[j]

    def chunk(way, kind, j, s):
        at = 4 * kind + j
        some = pl.ds(pl.multiple_of(s * sub, sub), sub)
        very_last = kind == LATE and j == 3 and s == 1
        return copy(
            rs_send.at[way, at, some, :],
            late_ref.at[way] if very_last else rs_recv.at[way, at, some, :],
            rs_ssem.at[0],
            rs_rsem.at[way, at, s],
            to[way],
        )

    def pass_on(kind, j, first=0, count=2):
        def one(s, _):
            some = pl.ds(pl.multiple_of(s * sub, sub), sub)
            for way in (RIGHT, LEFT):
                row = pl.multiple_of(s * half + (1 - way) * sub, sub)
                x = part[block_of(kind, j), pl.ds(row, sub), :]
                if j > 0:
                    chunk(way, kind, j - 1, s).wait_recv()
                    x = x + decode(rs_recv[way, 4 * kind + j - 1, some, :])
                rs_send[way, 4 * kind + j, some, :] = encode(x)
                chunk(way, kind, j, s).start()
            return 0

        if j == 3:
            one(0, 0)
            one(1, 0)
        else:
            lax.fori_loop(first, first + count, one, 0)

    def loss_copy(way, kind, j):
        at = 4 * kind + j
        return copy(
            loss_send.at[way, at],
            loss_recv.at[way, at],
            loss_ssem.at[0],
            loss_rsem.at[way, at],
            to[way],
        )

    def loss_on(kind, j):
        for way in (RIGHT, LEFT):
            x = loss_part[block_of(kind, j)]
            if j > 0:
                loss_copy(way, kind, j - 1).wait_recv()
                x = x + loss_recv[way, 4 * kind + j - 1]
            loss_send[way, 4 * kind + j] = x
            loss_copy(way, kind, j).start()

    for i in range(2):
        serve(i, 0)
        serve(i, 1)
    text_copy(1).wait_recv()
    text_copy(2).start()
    serve(2, 0)
    serve(2, 1)
    text_copy(0).wait_recv()
    text_copy(2).wait_recv()

    def work(k, _):
        @pl.when(k == 1)
        def _():
            serve(3, 0)

        @pl.when(k == 2)
        def _():
            serve(3, 1)

        @pl.when(k == 4)
        def _():
            serve(4, 0)
            serve(4, 1)

        @pl.when(k == 5)
        def _():
            loss_on(EARLY, 0)
            pass_on(EARLY, 0)

        @pl.when(k == 6)
        def _():
            serve(5, 0)
            serve(5, 1)

        tile(jnp.where(k < 5, k + 1, jnp.where(k == 5, 0, 6)), 0, rows, True)
        return 0

    lax.fori_loop(0, 7, work, 0)

    def farthest(s, _):
        for way in (RIGHT, LEFT):
            gather_wait(way, 6, s)
        tile(7, pl.multiple_of(s * half, half), half)
        pl.when(s == 1)(lambda: loss_on(LATE, 0))
        pass_on(LATE, 0, s, 1)
        return 0

    lax.fori_loop(0, 2, farthest, 0)

    def text_sums(b):
        sums[b] = tn(
            coefs[:, :, pl.ds(pl.multiple_of(b * rows, rows), rows)].reshape(RING * rows, rows),
            img[...].reshape(RING * rows, img.shape[2]),
        )

    def core_copy(i):
        return copy(sums.at[1 + 2 * i], core_recv.at[i], c_ssem.at[i], c_rsem.at[i], other_core)

    y_copy = copy(y_send, y_recv, y_ssem.at[0], y_rsem.at[0], other_y)

    def sums_work(k, _):
        b = jnp.where(k == 0, 3, jnp.where(k == 1, 1, jnp.where(k == 2, 2, 0)))
        text_sums(b)

        @pl.when(k == 0)
        def _():
            core_copy(1).start()

        @pl.when(k == 1)
        def _():
            core_copy(0).start()
            loss_on(EARLY, 1)
            pass_on(EARLY, 1)

        return 0

    lax.fori_loop(0, QUAD, sums_work, 0)
    loss_on(LATE, 1)
    pass_on(LATE, 1)
    core_copy(1).wait_recv()
    y_send[...] = encode(sums[2] + core_recv[1])
    y_copy.start()
    loss_on(EARLY, 2)
    pass_on(EARLY, 2, 0, 1)
    loss_on(LATE, 2)
    pass_on(LATE, 2)
    pass_on(EARLY, 2, 1, 1)
    core_copy(0).wait_recv()
    sums[0] += core_recv[0]
    loss_on(LATE, 3)
    pass_on(LATE, 3)

    def own_rows(way, kind, s):
        at = (half if (way == RIGHT) == (kind == EARLY) else 0) + s * sub
        return pl.ds(pl.multiple_of(at, sub), sub)

    def last(way, kind, s):
        some = pl.ds(pl.multiple_of(s * sub, sub), sub)
        chunk(way, kind, 3 - kind, s).wait_recv()
        at = own_rows(way, kind, s)
        return at, part[0, at, :] + decode(rs_recv[way, 4 * kind + 3 - kind, some, :])

    def add_early(s, _):
        for way in (RIGHT, LEFT):
            at, x = last(way, EARLY, s)
            part[0, at, :] = x
        return 0

    lax.fori_loop(0, 2, add_early, 0)
    y_copy.wait_recv()

    def finish_text(i, _):
        at = pl.ds(pl.multiple_of(i * sub, sub), sub)
        g = sums[0, at, :] + decode(y_recv[at, :])
        gt_ref[at, :] = unnormal(g, unit_t[at, :], inv_t[at, :], scale)
        return 0

    lax.fori_loop(0, 4, finish_text, 0)

    def lanes(way, kind):
        loss_copy(way, kind, 3 - kind).wait_recv()
        x = loss_recv[way, 4 * kind + 3 - kind]
        at = (1 - way) * sub
        return [x[:, s * half + at : s * half + at + sub] for s in range(2)]

    loss_ref[...] = (
        loss_part[0]
        + jnp.concatenate(lanes(RIGHT, LATE) + lanes(RIGHT, EARLY), axis=1)
        + jnp.concatenate(lanes(LEFT, EARLY) + lanes(LEFT, LATE), axis=1)
    )
    def all_sent(x, ssem, rsem):
        copy(x, x, ssem, rsem, to[RIGHT]).wait_send()

    all_sent(img.at[pl.ds(0, 7)], ag_ssem.at[0], ag_rsem.at[0, 0, 0])
    for i in range(3):
        text_copy(i).wait_send()
    for i in range(2):
        core_copy(i).wait_send()
    y_copy.wait_send()

    for way in (RIGHT, LEFT):
        at = own_rows(way, LATE, 1)
        gi_ref[at, :] = part[0, at, :]
    for way in (RIGHT, LEFT):
        at, g = last(way, LATE, 0)
        gi_ref[at, :] = unnormal(g, unit_i[at, :], inv_i[at, :], scale)
    for way in (RIGHT, LEFT):
        chunk(way, LATE, 3, 1).wait_recv()
    all_sent(rs_send, rs_ssem.at[0], rs_rsem.at[0, 0, 0])
    all_sent(loss_send, loss_ssem.at[0], loss_rsem.at[0, 0])


def write_out(
    loss_in, gi_in, gt_in, late, unit, inv, both, loss_out, gi_out, gt_out, row, rest, sem
):
    sub = late.shape[1]
    row[...] = loss_in[0]
    copies = [
        pltpu.make_async_copy(gt_in, gt_out, sem.at[0]),
        pltpu.make_async_copy(row, loss_out, sem.at[1]),
    ]
    for way in (RIGHT, LEFT):
        some = pl.ds(way * 2 * sub, sub)
        copies.append(pltpu.make_async_copy(gi_in.at[some, :], gi_out.at[some, :], sem.at[2 + way]))
    for c in copies:
        c.start()
    scale = both[0:1, 0:1]
    for way in (RIGHT, LEFT):
        some = pl.ds(way * 2 * sub + sub, sub)
        g = gi_in[some, :] + decode(late[way])
        rest[way] = unnormal(g, unit[some, :], inv[some, :], scale)
        c = pltpu.make_async_copy(rest.at[way], gi_out.at[some, :], sem.at[4 + way])
        c.start()
        copies.append(c)
    for c in copies:
        c.wait()


def per_device(image_embed, text_embed, logit_scale, logit_bias):
    rows, width = image_embed.shape
    half = rows // 2
    dma = pltpu.SemaphoreType.DMA
    vmem = pl.BlockSpec(memory_space=pltpu.VMEM)
    hbm = pl.BlockSpec(memory_space=pltpu.HBM)
    image_embed = pltpu.with_memory_space_constraint(image_embed, pltpu.HBM)
    text_embed = pltpu.with_memory_space_constraint(text_embed, pltpu.HBM)
    row = lax.broadcasted_iota(jnp.int32, (8, 128), 0)
    both = jnp.where(row == 0, logit_scale[0], logit_bias[0])
    anywhere = pl.BlockSpec(memory_space=pl.ANY)
    results = pl.pallas_call(
        kernel,
        out_shape=(
            pltpu.VMEM((1, rows), F32),
            pltpu.VMEM((rows, width), F32),
            pltpu.VMEM((rows, width), F32),
            pltpu.VMEM((2, rows // 4, width), BF16),
            pltpu.VMEM((rows, width), F32),
            pltpu.VMEM((rows, 128), F32),
        ),
        in_specs=[hbm, hbm, vmem],
        out_specs=(vmem,) * 6,
        scratch_shapes=[
            pltpu.VMEM((rows, width), BF16),
            pltpu.VMEM((rows, width), BF16),
            pltpu.VMEM((RING, rows, width), BF16),
            pltpu.VMEM((QUAD * rows, width), BF16),
            pltpu.VMEM((RING, rows, width), F32),
            pltpu.VMEM((RING, rows, QUAD * rows), BF16),
            pltpu.VMEM((QUAD, rows, width), F32),
            pltpu.VMEM((2, 7, half, width), BF16),
            pltpu.VMEM((2, 7, half, width), BF16),
            pltpu.VMEM((2, rows, width), F32),
            pltpu.VMEM((rows, width), BF16),
            pltpu.VMEM((rows, width), BF16),
            pltpu.VMEM((rows, width), F32),
            pltpu.VMEM((rows, 128), F32),
            pltpu.VMEM((RING, 1, rows), F32),
            pltpu.VMEM((2, 7, 1, rows), F32),
            pltpu.VMEM((2, 7, 1, rows), F32),
            dma((4,)),
            dma((1,)),
            dma((2, 7, 2)),
            dma((1,)),
            dma((2, 7, 2)),
            dma((1,)),
            dma((2, 7)),
            dma((3,)),
            dma((3,)),
            dma((2,)),
            dma((2,)),
            dma((1,)),
            dma((1,)),
        ],
        compiler_params=pltpu.CompilerParams(
            collective_id=0, has_side_effects=True, vmem_limit_bytes=48 * 2**20
        ),
        cost_estimate=pl.CostEstimate(
            flops=3 * 2 * 1024 * 512 * width, bytes_accessed=6 * rows * width, transcendentals=0
        ),
    )(image_embed, text_embed, both)
    return pl.pallas_call(
        write_out,
        out_shape=(
            jax.ShapeDtypeStruct((rows,), F32),
            jax.ShapeDtypeStruct((rows, width), F32),
            jax.ShapeDtypeStruct((rows, width), F32),
        ),
        in_specs=[vmem] * 7,
        out_specs=(anywhere, anywhere, anywhere),
        scratch_shapes=[pltpu.VMEM((rows,), F32), pltpu.VMEM((2, rows // 4, width), F32), dma((6,))],
        compiler_params=pltpu.CompilerParams(vmem_limit_bytes=4 * 2**20),
        cost_estimate=pl.CostEstimate(flops=0, bytes_accessed=16 * rows * width, transcendentals=0),
    )(*results, both)


def solution(mesh):
    placed = (P(("group", "blk"), None), P(("group", "blk"), None), P(), P())
    return jax.shard_map(
        per_device,
        mesh=mesh,
        in_specs=placed,
        out_specs=(P(("group", "blk")), P(("group", "blk"), None), P(("group", "blk"), None)),
        check_vma=False,
    )
```

```python
import functools

import jax
import jax.numpy as jnp
from jax import lax
from jax.experimental import pallas as pl
from jax.experimental.pallas import tpu as pltpu
from jax.sharding import PartitionSpec as P

MESH = pl.DeviceIdType.MESH
F32 = jnp.float32
BF16 = jnp.bfloat16

RING = 8
QUAD = 4
RIGHT, LEFT = 0, 1
LATE, EARLY = 0, 1
EPS = 1e-06
CODE = 2.0**13
TINY = 2.0**-126


def encode(x):
    a = x * CODE
    a2 = a * a
    return (a2 * a2 * a).astype(BF16)


def decode(y):
    y = y.astype(F32)
    root = jnp.exp(jnp.log(jnp.maximum(jnp.abs(y), TINY)) * 0.2) * (1.0 / CODE)
    return jnp.where(y < 0, -root, root)


def nt(a, b):
    return lax.dot_general(a, b, (((1,), (1,)), ((), ())), preferred_element_type=F32)


def tn(a, b):
    return lax.dot_general(a, b, (((0,), (0,)), ((), ())), preferred_element_type=F32)


def unnormal(g, u, inv, scale):
    along = jnp.sum(u * g, axis=1, keepdims=True)
    return (g - u * along) * (inv[:, 0:1] * scale)


def kernel(
    img_hbm,
    txt_hbm,
    both_ref,
    loss_ref,
    gi_ref,
    gt_ref,
    late_ref,
    unit_i,
    inv_i,
    img_ref,
    txt_ref,
    img,
    txt,
    part,
    coefs,
    sums,
    rs_send,
    rs_recv,
    core_recv,
    y_send,
    y_recv,
    unit_t,
    inv_t,
    loss_part,
    loss_send,
    loss_recv,
    in_sem,
    ag_ssem,
    ag_rsem,
    rs_ssem,
    rs_rsem,
    loss_ssem,
    loss_rsem,
    t_ssem,
    t_rsem,
    c_ssem,
    c_rsem,
    y_ssem,
    y_rsem,
):
    rows = img_ref.shape[0]
    half = rows // 2
    sub = half // 2
    me = lax.axis_index("blk")
    n = RING * QUAD
    to = (lax.rem(me + QUAD, n), lax.rem(me + n - QUAD, n))
    other_core = me + 1 - 2 * lax.rem(me, 2)
    other_y = me + 2 - 4 * lax.rem(lax.div(me, 2), 2)

    def copy(src, dst, ssem, rsem, device):
        return pltpu.make_async_remote_copy(
            src_ref=src,
            dst_ref=dst,
            send_sem=ssem,
            recv_sem=rsem,
            device_id={"blk": device},
            device_id_type=MESH,
        )

    barrier = pltpu.get_barrier_semaphore()
    for peer in (*to, other_core, other_y):
        pl.semaphore_signal(barrier, inc=1, device_id={"blk": peer}, device_id_type=MESH)

    def load(i):
        src, dst = ((img_hbm, img_ref), (txt_hbm, txt_ref))[i // 2]
        some = pl.ds(i % 2 * half, half)
        return pltpu.make_async_copy(src.at[some, :], dst.at[some, :], in_sem.at[i])

    for i in range(4):
        load(i).start()

    def normalize(src, at, size, unit, inv, out):
        values = src[pl.ds(at, size), :].astype(F32)
        norm = jnp.sqrt(jnp.sum(values * values, axis=1, keepdims=True) + EPS)
        inverse = 1.0 / norm
        u = values * inverse
        unit[pl.ds(at, size), :] = u
        inv[pl.ds(at, size), :] = jnp.broadcast_to(inverse, (size, 128))
        out[pl.ds(at, size), :] = u.astype(BF16)

    def place(way, i, s):
        side = way if i < 6 else 1 - way
        return s * half + side * sub

    def gather(way, i, s):
        if i < 2:
            piece = i if way == RIGHT else 1 - i
            src = img.at[0, pl.ds(piece * half + s * sub, sub), :]
        else:
            src = img.at[i - 1, pl.ds(place(way, i - 2, s), sub), :]
        dst = img.at[i + 1, pl.ds(place(way, i, s), sub), :]
        return copy(src, dst, ag_ssem.at[0], ag_rsem.at[way, i, s], to[way])

    for i in range(2):
        load(i).wait()
        normalize(img_ref, i * half, half, unit_i, inv_i, img.at[0])
        if i == 0:
            pl.semaphore_wait(barrier, 4)
        for s in range(2):
            gather(i, 0, s).start()
    for s in range(2):
        for way in (RIGHT, LEFT):
            gather(way, 1, s).start()

    for i in range(2):
        load(2 + i).wait()
        normalize(txt_ref, i * half, half, unit_t, inv_t, txt)

    scale = both_ref[0:1, 0:1]
    bias = both_ref[0:1, 1:2]

    def text_copy(i):
        src = (0, 0, 2)[i]
        dst = (1, 2, 3)[i]
        device = (other_core, other_y, other_core)[i]
        return copy(
            txt.at[pl.ds(src * rows, rows), :],
            txt.at[pl.ds(dst * rows, rows), :],
            t_ssem.at[i],
            t_rsem.at[i],
            device,
        )

    text_copy(1).start()
    text_copy(0).start()

    def tile(block, at, size, maybe_own=False):
        some = pl.ds(at, size)
        wide = 2 * rows
        total = jnp.zeros((size, rows), F32)
        for h in range(2):
            m = nt(img[block, some, :], txt[pl.ds(h * wide, wide), :]) * scale + bias
            if maybe_own and h == 0:
                row = lax.broadcasted_iota(jnp.int32, m.shape, 0)
                col = lax.broadcasted_iota(jnp.int32, m.shape, 1)
                eye = row + jnp.where(block == 0, 0, 2 * wide) == col
                m = jnp.where(eye, -m, m)
            e = jnp.exp(-jnp.abs(m))
            soft = jnp.maximum(m, 0.0) + jnp.log1p(e)
            r = 1.0 / (1.0 + e)
            coef = jnp.where(m >= 0, r, e * r)
            if maybe_own and h == 0:
                coef = jnp.where(eye, -coef, coef)
            total = total + soft[:, :rows] + soft[:, rows:]
            coefs[block, some, pl.ds(h * wide, wide)] = coef.astype(BF16)
        part[block, some, :] = jnp.dot(
            coefs[block, some, :], txt[...], preferred_element_type=F32
        )
        if size < rows:
            total = jnp.concatenate([total, total], axis=0)
        across = jnp.sum(total.T, axis=0, keepdims=True)
        if size < rows:
            lane = lax.broadcasted_iota(jnp.int32, (1, rows), 1)
            across = jnp.where(lane < at, loss_part[block], across)
        loss_part[block] = across

    def serve(i, s):
        for way in (RIGHT, LEFT):
            gather(way, i, s).wait_recv()
            if i < 5:
                gather(way, i + 2, s).start()

    def gather_wait(way, i, s):
        row = pl.multiple_of(place(way, i, s), sub)
        some = img.at[i + 1, pl.ds(row, sub), :]
        copy(some, some, ag_ssem.at[0], ag_rsem.at[way, i, s], to[way]).wait_recv()

    def block_of(kind, j):
        return (7, 6, 4, 2)[j] if kind == LATE else (5, 3, 1)[j]

    def whole(kind, j):
        return kind == EARLY and j < 2

    def chunk(way, kind, j, s):
        at = 4 * kind + j
        if whole(kind, j):
            some, s = pl.ds(0, half), 0
        else:
            some = pl.ds(pl.multiple_of(s * sub, sub), sub)
        very_last = kind == LATE and j == 3 and s == 1
        return copy(
            rs_send.at[way, at, some, :],
            late_ref.at[way] if very_last else rs_recv.at[way, at, some, :],
            rs_ssem.at[0],
            rs_rsem.at[way, at, s],
            to[way],
        )

    def add_to(way, kind, j, s):
        some = pl.ds(pl.multiple_of(s * sub, sub), sub)
        row = pl.multiple_of(s * half + (1 - way) * sub, sub)
        x = part[block_of(kind, j), pl.ds(row, sub), :]
        if j > 0:
            x = x + decode(rs_recv[way, 4 * kind + j - 1, some, :])
        rs_send[way, 4 * kind + j, some, :] = encode(x)

    def pass_on(kind, j, first=0, count=2):
        def one(s, _):
            for way in (RIGHT, LEFT):
                if j > 0 and not (whole(kind, j - 1) and first > 0):
                    chunk(way, kind, j - 1, s).wait_recv()
                add_to(way, kind, j, s)
                chunk(way, kind, j, s).start()
            return 0

        if whole(kind, j):
            for way in (RIGHT, LEFT):
                if j > 0:
                    chunk(way, kind, j - 1, 0).wait_recv()
                for s in range(2):
                    add_to(way, kind, j, s)
                chunk(way, kind, j, 0).start()
        elif j == 3:
            one(0, 0)
            one(1, 0)
        else:
            lax.fori_loop(first, first + count, one, 0)

    def loss_copy(way, j):
        return copy(
            loss_send.at[way, j],
            loss_recv.at[way, j],
            loss_ssem.at[0],
            loss_rsem.at[way, j],
            to[way],
        )

    def loss_on(j):
        for way in (RIGHT, LEFT):
            late = loss_part[block_of(LATE, j)]
            early = jnp.zeros_like(late)
            if j > 0:
                loss_copy(way, j - 1).wait_recv()
                late = late + loss_recv[way, j - 1, 0:1, :]
                early = loss_part[block_of(EARLY, j - 1)] + loss_recv[way, j - 1, 1:2, :]
            loss_send[way, j, 0:1, :] = late
            loss_send[way, j, 1:2, :] = early
            loss_copy(way, j).start()

    for i in range(2):
        serve(i, 0)
        serve(i, 1)
    text_copy(1).wait_recv()
    text_copy(2).start()
    serve(2, 0)
    serve(2, 1)
    text_copy(0).wait_recv()
    text_copy(2).wait_recv()

    def work(k, _):
        @pl.when(k == 1)
        def _():
            serve(3, 0)

        @pl.when(k == 2)
        def _():
            serve(3, 1)

        @pl.when(k == 4)
        def _():
            serve(4, 0)
            serve(4, 1)

        @pl.when(k == 5)
        def _():
            pass_on(EARLY, 0)

        @pl.when(k == 6)
        def _():
            serve(5, 0)
            serve(5, 1)

        tile(jnp.where(k < 5, k + 1, jnp.where(k == 5, 0, 6)), 0, rows, True)
        return 0

    lax.fori_loop(0, 7, work, 0)

    def farthest(s, _):
        for way in (RIGHT, LEFT):
            gather_wait(way, 6, s)
        tile(7, pl.multiple_of(s * half, half), half)
        pl.when(s == 1)(lambda: loss_on(0))
        pass_on(LATE, 0, s, 1)
        return 0

    lax.fori_loop(0, 2, farthest, 0)

    def text_sums(b):
        sums[b] = tn(
            coefs[:, :, pl.ds(pl.multiple_of(b * rows, rows), rows)].reshape(RING * rows, rows),
            img[...].reshape(RING * rows, img.shape[2]),
        )

    def core_copy(i):
        return copy(sums.at[1 + 2 * i], core_recv.at[i], c_ssem.at[i], c_rsem.at[i], other_core)

    y_copy = copy(y_send, y_recv, y_ssem.at[0], y_rsem.at[0], other_y)

    def sums_work(k, _):
        b = jnp.where(k == 0, 3, jnp.where(k == 1, 1, jnp.where(k == 2, 2, 0)))
        text_sums(b)

        @pl.when(k == 0)
        def _():
            core_copy(1).start()

        @pl.when(k == 1)
        def _():
            core_copy(0).start()
            pass_on(EARLY, 1)

        return 0

    lax.fori_loop(0, QUAD, sums_work, 0)
    loss_on(1)
    pass_on(LATE, 1)
    core_copy(1).wait_recv()
    y_send[...] = encode(sums[2] + core_recv[1])
    y_copy.start()
    pass_on(EARLY, 2, 0, 1)
    loss_on(2)
    pass_on(LATE, 2)
    pass_on(EARLY, 2, 1, 1)
    core_copy(0).wait_recv()
    sums[0] += core_recv[0]
    loss_on(3)
    pass_on(LATE, 3)

    def own_rows(way, kind, s):
        at = (half if (way == RIGHT) == (kind == EARLY) else 0) + s * sub
        return pl.ds(pl.multiple_of(at, sub), sub)

    def last(way, kind, s):
        some = pl.ds(pl.multiple_of(s * sub, sub), sub)
        chunk(way, kind, 3 - kind, s).wait_recv()
        at = own_rows(way, kind, s)
        return at, part[0, at, :] + decode(rs_recv[way, 4 * kind + 3 - kind, some, :])

    def add_early(s, _):
        for way in (RIGHT, LEFT):
            at, x = last(way, EARLY, s)
            part[0, at, :] = x
        return 0

    lax.fori_loop(0, 2, add_early, 0)
    y_copy.wait_recv()

    def finish_text(i, _):
        at = pl.ds(pl.multiple_of(i * sub, sub), sub)
        g = sums[0, at, :] + decode(y_recv[at, :])
        gt_ref[at, :] = unnormal(g, unit_t[at, :], inv_t[at, :], scale)
        return 0

    lax.fori_loop(0, 4, finish_text, 0)

    def lanes(way, kind):
        x = loss_recv[way, 3, kind : kind + 1, :]
        at = (1 - way) * sub
        return [x[:, s * half + at : s * half + at + sub] for s in range(2)]

    for way in (RIGHT, LEFT):
        loss_copy(way, 3).wait_recv()
    loss_ref[...] = (
        loss_part[0]
        + jnp.concatenate(lanes(RIGHT, LATE) + lanes(RIGHT, EARLY), axis=1)
        + jnp.concatenate(lanes(LEFT, EARLY) + lanes(LEFT, LATE), axis=1)
    )
    def all_sent(x, ssem, rsem):
        copy(x, x, ssem, rsem, to[RIGHT]).wait_send()

    all_sent(img.at[pl.ds(0, 7)], ag_ssem.at[0], ag_rsem.at[0, 0, 0])
    for i in range(3):
        text_copy(i).wait_send()
    for i in range(2):
        core_copy(i).wait_send()
    y_copy.wait_send()

    for way in (RIGHT, LEFT):
        at = own_rows(way, LATE, 1)
        gi_ref[at, :] = part[0, at, :]
    for way in (RIGHT, LEFT):
        at, g = last(way, LATE, 0)
        gi_ref[at, :] = unnormal(g, unit_i[at, :], inv_i[at, :], scale)
    for way in (RIGHT, LEFT):
        chunk(way, LATE, 3, 1).wait_recv()
    all_sent(rs_send, rs_ssem.at[0], rs_rsem.at[0, 0, 0])
    all_sent(loss_send, loss_ssem.at[0], loss_rsem.at[0, 0])


def write_out(
    loss_in, gi_in, gt_in, late, unit, inv, both, loss_out, gi_out, gt_out, row, rest, sem
):
    sub = late.shape[1]
    row[...] = loss_in[0]
    copies = [
        pltpu.make_async_copy(gt_in, gt_out, sem.at[0]),
        pltpu.make_async_copy(row, loss_out, sem.at[1]),
    ]
    for way in (RIGHT, LEFT):
        some = pl.ds(way * 2 * sub, sub)
        copies.append(pltpu.make_async_copy(gi_in.at[some, :], gi_out.at[some, :], sem.at[2 + way]))
    for c in copies:
        c.start()
    scale = both[0:1, 0:1]
    for way in (RIGHT, LEFT):
        some = pl.ds(way * 2 * sub + sub, sub)
        g = gi_in[some, :] + decode(late[way])
        rest[way] = unnormal(g, unit[some, :], inv[some, :], scale)
        c = pltpu.make_async_copy(rest.at[way], gi_out.at[some, :], sem.at[4 + way])
        c.start()
        copies.append(c)
    for c in copies:
        c.wait()


def per_device(image_embed, text_embed, logit_scale, logit_bias):
    rows, width = image_embed.shape
    half = rows // 2
    dma = pltpu.SemaphoreType.DMA
    vmem = pl.BlockSpec(memory_space=pltpu.VMEM)
    hbm = pl.BlockSpec(memory_space=pltpu.HBM)
    image_embed = pltpu.with_memory_space_constraint(image_embed, pltpu.HBM)
    text_embed = pltpu.with_memory_space_constraint(text_embed, pltpu.HBM)
    lane = lax.broadcasted_iota(jnp.int32, (1, 128), 1)
    both = jnp.where(lane == 0, logit_scale[0], logit_bias[0])
    anywhere = pl.BlockSpec(memory_space=pl.ANY)
    results = pl.pallas_call(
        kernel,
        out_shape=(
            pltpu.VMEM((1, rows), F32),
            pltpu.VMEM((rows, width), F32),
            pltpu.VMEM((rows, width), F32),
            pltpu.VMEM((2, rows // 4, width), BF16),
            pltpu.VMEM((rows, width), F32),
            pltpu.VMEM((rows, 128), F32),
        ),
        in_specs=[hbm, hbm, vmem],
        out_specs=(vmem,) * 6,
        scratch_shapes=[
            pltpu.VMEM((rows, width), BF16),
            pltpu.VMEM((rows, width), BF16),
            pltpu.VMEM((RING, rows, width), BF16),
            pltpu.VMEM((QUAD * rows, width), BF16),
            pltpu.VMEM((RING, rows, width), F32),
            pltpu.VMEM((RING, rows, QUAD * rows), BF16),
            pltpu.VMEM((QUAD, rows, width), F32),
            pltpu.VMEM((2, 7, half, width), BF16),
            pltpu.VMEM((2, 7, half, width), BF16),
            pltpu.VMEM((2, rows, width), F32),
            pltpu.VMEM((rows, width), BF16),
            pltpu.VMEM((rows, width), BF16),
            pltpu.VMEM((rows, width), F32),
            pltpu.VMEM((rows, 128), F32),
            pltpu.VMEM((RING, 1, rows), F32),
            pltpu.VMEM((2, 4, 2, rows), F32),
            pltpu.VMEM((2, 4, 2, rows), F32),
            dma((4,)),
            dma((1,)),
            dma((2, 7, 2)),
            dma((1,)),
            dma((2, 7, 2)),
            dma((1,)),
            dma((2, 4)),
            dma((3,)),
            dma((3,)),
            dma((2,)),
            dma((2,)),
            dma((1,)),
            dma((1,)),
        ],
        compiler_params=pltpu.CompilerParams(
            collective_id=0, has_side_effects=True, vmem_limit_bytes=48 * 2**20
        ),
        cost_estimate=pl.CostEstimate(
            flops=3 * 2 * 1024 * 512 * width, bytes_accessed=6 * rows * width, transcendentals=0
        ),
    )(image_embed, text_embed, both)
    return pl.pallas_call(
        write_out,
        out_shape=(
            jax.ShapeDtypeStruct((rows,), F32),
            jax.ShapeDtypeStruct((rows, width), F32),
            jax.ShapeDtypeStruct((rows, width), F32),
        ),
        in_specs=[vmem] * 7,
        out_specs=(anywhere, anywhere, anywhere),
        scratch_shapes=[pltpu.VMEM((rows,), F32), pltpu.VMEM((2, rows // 4, width), F32), dma((6,))],
        compiler_params=pltpu.CompilerParams(vmem_limit_bytes=4 * 2**20),
        cost_estimate=pl.CostEstimate(flops=0, bytes_accessed=16 * rows * width, transcendentals=0),
    )(*results, both)


def solution(mesh):
    placed = (P(("group", "blk"), None), P(("group", "blk"), None), P(), P())
    return jax.shard_map(
        per_device,
        mesh=mesh,
        in_specs=placed,
        out_specs=(P(("group", "blk")), P(("group", "blk"), None), P(("group", "blk"), None)),
        check_vma=False,
    )
```

```python
import functools

import jax
import jax.numpy as jnp
from jax import lax
from jax.experimental import pallas as pl
from jax.experimental.pallas import tpu as pltpu
from jax.sharding import PartitionSpec as P

MESH = pl.DeviceIdType.MESH
F32 = jnp.float32
BF16 = jnp.bfloat16

RING = 8
QUAD = 4
RIGHT, LEFT = 0, 1
LATE, EARLY = 0, 1
EPS = 1e-06
CODE = 2.0**13
TINY = 2.0**-126


def encode(x):
    a = x * CODE
    a2 = a * a
    return (a2 * a2 * a).astype(BF16)


def decode(y):
    y = y.astype(F32)
    root = jnp.exp(jnp.log(jnp.maximum(jnp.abs(y), TINY)) * 0.2) * (1.0 / CODE)
    return jnp.where(y < 0, -root, root)


def nt(a, b):
    return lax.dot_general(a, b, (((1,), (1,)), ((), ())), preferred_element_type=F32)


def tn(a, b):
    return lax.dot_general(a, b, (((0,), (0,)), ((), ())), preferred_element_type=F32)


def unnormal(g, u, inv, scale):
    along = jnp.sum(u * g, axis=1, keepdims=True)
    return (g - u * along) * (inv[:, 0:1] * scale)


def kernel(
    img_hbm,
    txt_hbm,
    both_ref,
    loss_ref,
    gi_ref,
    gt_ref,
    late_ref,
    unit_i,
    inv_i,
    img_ref,
    txt_ref,
    img,
    txt,
    part,
    coefs,
    sums,
    rs_send,
    rs_recv,
    core_recv,
    y_send,
    y_recv,
    unit_t,
    inv_t,
    loss_part,
    loss_send,
    loss_recv,
    in_sem,
    ag_ssem,
    ag_rsem,
    rs_ssem,
    rs_rsem,
    loss_ssem,
    loss_rsem,
    t_ssem,
    t_rsem,
    c_ssem,
    c_rsem,
    y_ssem,
    y_rsem,
):
    rows = img_ref.shape[0]
    half = rows // 2
    sub = half // 2
    me = lax.axis_index("blk")
    n = RING * QUAD
    to = (lax.rem(me + QUAD, n), lax.rem(me + n - QUAD, n))
    other_core = me + 1 - 2 * lax.rem(me, 2)
    other_y = me + 2 - 4 * lax.rem(lax.div(me, 2), 2)

    def copy(src, dst, ssem, rsem, device):
        return pltpu.make_async_remote_copy(
            src_ref=src,
            dst_ref=dst,
            send_sem=ssem,
            recv_sem=rsem,
            device_id={"blk": device},
            device_id_type=MESH,
        )

    barrier = pltpu.get_barrier_semaphore()
    for peer in (*to, other_core, other_y):
        pl.semaphore_signal(barrier, inc=1, device_id={"blk": peer}, device_id_type=MESH)

    def load(i):
        src, dst = ((img_hbm, img_ref), (txt_hbm, txt_ref))[i // 2]
        some = pl.ds(i % 2 * half, half)
        return pltpu.make_async_copy(src.at[some, :], dst.at[some, :], in_sem.at[i])

    for i in range(4):
        load(i).start()

    def normalize(src, at, size, unit, inv, out):
        values = src[pl.ds(at, size), :].astype(F32)
        norm = jnp.sqrt(jnp.sum(values * values, axis=1, keepdims=True) + EPS)
        inverse = 1.0 / norm
        u = values * inverse
        unit[pl.ds(at, size), :] = u
        inv[pl.ds(at, size), :] = jnp.broadcast_to(inverse, (size, 128))
        out[pl.ds(at, size), :] = u.astype(BF16)

    def place(way, i, s):
        side = way if i < 6 else 1 - way
        return s * half + side * sub

    def gather(way, i, s):
        if i < 2:
            piece = i if way == RIGHT else 1 - i
            src = img.at[0, pl.ds(piece * half + s * sub, sub), :]
        else:
            src = img.at[i - 1, pl.ds(place(way, i - 2, s), sub), :]
        dst = img.at[i + 1, pl.ds(place(way, i, s), sub), :]
        return copy(src, dst, ag_ssem.at[0], ag_rsem.at[way, i, s], to[way])

    for i in range(2):
        load(i).wait()
        normalize(img_ref, i * half, half, unit_i, inv_i, img.at[0])
        if i == 0:
            pl.semaphore_wait(barrier, 4)
        for s in range(2):
            gather(i, 0, s).start()
    for s in range(2):
        for way in (RIGHT, LEFT):
            gather(way, 1, s).start()

    for i in range(2):
        load(2 + i).wait()
        normalize(txt_ref, i * half, half, unit_t, inv_t, txt)

    scale = both_ref[0:1, 0:1]
    bias = both_ref[0:1, 1:2]

    def text_copy(i):
        src = (0, 0, 2)[i]
        dst = (1, 2, 3)[i]
        device = (other_core, other_y, other_core)[i]
        return copy(
            txt.at[pl.ds(src * rows, rows), :],
            txt.at[pl.ds(dst * rows, rows), :],
            t_ssem.at[i],
            t_rsem.at[i],
            device,
        )

    text_copy(1).start()
    text_copy(0).start()

    def tile(block, at, size, maybe_own=False):
        some = pl.ds(at, size)
        wide = 2 * rows
        total = jnp.zeros((size, rows), F32)
        for h in range(2):
            m = nt(img[block, some, :], txt[pl.ds(h * wide, wide), :]) * scale + bias
            if maybe_own and h == 0:
                row = lax.broadcasted_iota(jnp.int32, m.shape, 0)
                col = lax.broadcasted_iota(jnp.int32, m.shape, 1)
                eye = row + jnp.where(block == 0, 0, 2 * wide) == col
                m = jnp.where(eye, -m, m)
            e = jnp.exp(-jnp.abs(m))
            soft = jnp.maximum(m, 0.0) + jnp.log1p(e)
            r = 1.0 / (1.0 + e)
            coef = jnp.where(m >= 0, r, e * r)
            if maybe_own and h == 0:
                coef = jnp.where(eye, -coef, coef)
            total = total + soft[:, :rows] + soft[:, rows:]
            coefs[block, some, pl.ds(h * wide, wide)] = coef.astype(BF16)
        part[block, some, :] = jnp.dot(
            coefs[block, some, :], txt[...], preferred_element_type=F32
        )
        if size < rows:
            total = jnp.concatenate([total, total], axis=0)
        across = jnp.sum(total.T, axis=0, keepdims=True)
        if size < rows:
            lane = lax.broadcasted_iota(jnp.int32, (1, rows), 1)
            across = jnp.where(lane < at, loss_part[block], across)
        loss_part[block] = across

    def serve(i, s):
        for way in (RIGHT, LEFT):
            gather(way, i, s).wait_recv()
            if i < 5:
                gather(way, i + 2, s).start()

    def gather_wait(way, i, s):
        row = pl.multiple_of(place(way, i, s), sub)
        some = img.at[i + 1, pl.ds(row, sub), :]
        copy(some, some, ag_ssem.at[0], ag_rsem.at[way, i, s], to[way]).wait_recv()

    def block_of(kind, j):
        return (7, 6, 4, 2)[j] if kind == LATE else (5, 3, 1)[j]

    def chunk(way, kind, j, s):
        at = 4 * kind + j
        some = pl.ds(pl.multiple_of(s * sub, sub), sub)
        very_last = kind == LATE and j == 3 and s == 1
        return copy(
            rs_send.at[way, at, some, :],
            late_ref.at[way] if very_last else rs_recv.at[way, at, some, :],
            rs_ssem.at[0],
            rs_rsem.at[way, at, s],
            to[way],
        )

    def pass_on(kind, j, first=0, count=2):
        def one(s, _):
            some = pl.ds(pl.multiple_of(s * sub, sub), sub)
            for way in (RIGHT, LEFT):
                row = pl.multiple_of(s * half + (1 - way) * sub, sub)
                x = part[block_of(kind, j), pl.ds(row, sub), :]
                if j > 0:
                    chunk(way, kind, j - 1, s).wait_recv()
                    x = x + decode(rs_recv[way, 4 * kind + j - 1, some, :])
                rs_send[way, 4 * kind + j, some, :] = encode(x)
                chunk(way, kind, j, s).start()
            return 0

        if j == 3:
            one(0, 0)
            one(1, 0)
        else:
            lax.fori_loop(first, first + count, one, 0)

    def loss_copy(way, kind, j):
        at = 4 * kind + j
        return copy(
            loss_send.at[way, at],
            loss_recv.at[way, at],
            loss_ssem.at[0],
            loss_rsem.at[way, at],
            to[way],
        )

    def loss_on(kind, j):
        for way in (RIGHT, LEFT):
            x = loss_part[block_of(kind, j)]
            if j > 0:
                loss_copy(way, kind, j - 1).wait_recv()
                x = x + loss_recv[way, 4 * kind + j - 1]
            loss_send[way, 4 * kind + j] = x
            loss_copy(way, kind, j).start()

    for i in range(2):
        serve(i, 0)
        serve(i, 1)
    text_copy(1).wait_recv()
    text_copy(2).start()
    serve(2, 0)
    serve(2, 1)
    text_copy(0).wait_recv()
    text_copy(2).wait_recv()

    def work(k, _):
        @pl.when(k == 1)
        def _():
            serve(3, 0)

        @pl.when(k == 2)
        def _():
            serve(3, 1)

        @pl.when(k == 4)
        def _():
            serve(4, 0)
            serve(4, 1)

        @pl.when(k == 5)
        def _():
            loss_on(EARLY, 0)
            pass_on(EARLY, 0)

        @pl.when(k == 6)
        def _():
            serve(5, 0)
            serve(5, 1)

        tile(jnp.where(k < 5, k + 1, jnp.where(k == 5, 0, 6)), 0, rows, True)
        return 0

    lax.fori_loop(0, 7, work, 0)

    def farthest(s, _):
        for way in (RIGHT, LEFT):
            gather_wait(way, 6, s)
        tile(7, pl.multiple_of(s * half, half), half)
        pl.when(s == 1)(lambda: loss_on(LATE, 0))
        pass_on(LATE, 0, s, 1)
        return 0

    lax.fori_loop(0, 2, farthest, 0)

    def text_sums(b):
        sums[b] = tn(
            coefs[:, :, pl.ds(pl.multiple_of(b * rows, rows), rows)].reshape(RING * rows, rows),
            img[...].reshape(RING * rows, img.shape[2]),
        )

    def core_copy(i):
        return copy(sums.at[1 + 2 * i], core_recv.at[i], c_ssem.at[i], c_rsem.at[i], other_core)

    y_copy = copy(y_send, y_recv, y_ssem.at[0], y_rsem.at[0], other_y)

    def sums_work(k, _):
        b = jnp.where(k == 0, 3, jnp.where(k == 1, 1, jnp.where(k == 2, 2, 0)))
        text_sums(b)

        @pl.when(k == 0)
        def _():
            core_copy(1).start()

        @pl.when(k == 1)
        def _():
            core_copy(0).start()
            loss_on(EARLY, 1)
            pass_on(EARLY, 1, 0, 1)

        return 0

    lax.fori_loop(0, QUAD, sums_work, 0)
    loss_on(LATE, 1)
    pass_on(LATE, 1)
    pass_on(EARLY, 1, 1, 1)
    core_copy(1).wait_recv()
    y_send[...] = encode(sums[2] + core_recv[1])
    y_copy.start()
    loss_on(EARLY, 2)
    pass_on(EARLY, 2, 0, 1)
    loss_on(LATE, 2)
    pass_on(LATE, 2)
    pass_on(EARLY, 2, 1, 1)
    core_copy(0).wait_recv()
    sums[0] += core_recv[0]
    loss_on(LATE, 3)
    pass_on(LATE, 3)

    def own_rows(way, kind, s):
        at = (half if (way == RIGHT) == (kind == EARLY) else 0) + s * sub
        return pl.ds(pl.multiple_of(at, sub), sub)

    def last(way, kind, s):
        some = pl.ds(pl.multiple_of(s * sub, sub), sub)
        chunk(way, kind, 3 - kind, s).wait_recv()
        at = own_rows(way, kind, s)
        return at, part[0, at, :] + decode(rs_recv[way, 4 * kind + 3 - kind, some, :])

    def add_early(s, _):
        for way in (RIGHT, LEFT):
            at, x = last(way, EARLY, s)
            part[0, at, :] = x
        return 0

    lax.fori_loop(0, 2, add_early, 0)
    y_copy.wait_recv()

    def finish_text(i, _):
        at = pl.ds(pl.multiple_of(i * sub, sub), sub)
        g = sums[0, at, :] + decode(y_recv[at, :])
        gt_ref[at, :] = unnormal(g, unit_t[at, :], inv_t[at, :], scale)
        return 0

    lax.fori_loop(0, 4, finish_text, 0)

    def lanes(way, kind):
        loss_copy(way, kind, 3 - kind).wait_recv()
        x = loss_recv[way, 4 * kind + 3 - kind]
        at = (1 - way) * sub
        return [x[:, s * half + at : s * half + at + sub] for s in range(2)]

    loss_ref[...] = (
        loss_part[0]
        + jnp.concatenate(lanes(RIGHT, LATE) + lanes(RIGHT, EARLY), axis=1)
        + jnp.concatenate(lanes(LEFT, EARLY) + lanes(LEFT, LATE), axis=1)
    )
    def all_sent(x, ssem, rsem):
        copy(x, x, ssem, rsem, to[RIGHT]).wait_send()

    all_sent(img.at[pl.ds(0, 7)], ag_ssem.at[0], ag_rsem.at[0, 0, 0])
    for i in range(3):
        text_copy(i).wait_send()
    for i in range(2):
        core_copy(i).wait_send()
    y_copy.wait_send()

    for way in (RIGHT, LEFT):
        at = own_rows(way, LATE, 1)
        gi_ref[at, :] = part[0, at, :]
    for way in (RIGHT, LEFT):
        at, g = last(way, LATE, 0)
        gi_ref[at, :] = unnormal(g, unit_i[at, :], inv_i[at, :], scale)
    for way in (RIGHT, LEFT):
        chunk(way, LATE, 3, 1).wait_recv()
    all_sent(rs_send, rs_ssem.at[0], rs_rsem.at[0, 0, 0])
    all_sent(loss_send, loss_ssem.at[0], loss_rsem.at[0, 0])


def write_out(
    loss_in, gi_in, gt_in, late, unit, inv, both, loss_out, gi_out, gt_out, row, rest, sem
):
    sub = late.shape[1]
    row[...] = loss_in[0]
    copies = [
        pltpu.make_async_copy(gt_in, gt_out, sem.at[0]),
        pltpu.make_async_copy(row, loss_out, sem.at[1]),
    ]
    for way in (RIGHT, LEFT):
        some = pl.ds(way * 2 * sub, sub)
        copies.append(pltpu.make_async_copy(gi_in.at[some, :], gi_out.at[some, :], sem.at[2 + way]))
    for c in copies:
        c.start()
    scale = both[0:1, 0:1]
    for way in (RIGHT, LEFT):
        some = pl.ds(way * 2 * sub + sub, sub)
        g = gi_in[some, :] + decode(late[way])
        rest[way] = unnormal(g, unit[some, :], inv[some, :], scale)
        c = pltpu.make_async_copy(rest.at[way], gi_out.at[some, :], sem.at[4 + way])
        c.start()
        copies.append(c)
    for c in copies:
        c.wait()


def per_device(image_embed, text_embed, logit_scale, logit_bias):
    rows, width = image_embed.shape
    half = rows // 2
    dma = pltpu.SemaphoreType.DMA
    vmem = pl.BlockSpec(memory_space=pltpu.VMEM)
    hbm = pl.BlockSpec(memory_space=pltpu.HBM)
    image_embed = pltpu.with_memory_space_constraint(image_embed, pltpu.HBM)
    text_embed = pltpu.with_memory_space_constraint(text_embed, pltpu.HBM)
    lane = lax.broadcasted_iota(jnp.int32, (1, 128), 1)
    both = jnp.where(lane == 0, logit_scale[0], logit_bias[0])
    anywhere = pl.BlockSpec(memory_space=pl.ANY)
    results = pl.pallas_call(
        kernel,
        out_shape=(
            pltpu.VMEM((1, rows), F32),
            pltpu.VMEM((rows, width), F32),
            pltpu.VMEM((rows, width), F32),
            pltpu.VMEM((2, rows // 4, width), BF16),
            pltpu.VMEM((rows, width), F32),
            pltpu.VMEM((rows, 128), F32),
        ),
        in_specs=[hbm, hbm, vmem],
        out_specs=(vmem,) * 6,
        scratch_shapes=[
            pltpu.VMEM((rows, width), BF16),
            pltpu.VMEM((rows, width), BF16),
            pltpu.VMEM((RING, rows, width), BF16),
            pltpu.VMEM((QUAD * rows, width), BF16),
            pltpu.VMEM((RING, rows, width), F32),
            pltpu.VMEM((RING, rows, QUAD * rows), BF16),
            pltpu.VMEM((QUAD, rows, width), F32),
            pltpu.VMEM((2, 7, half, width), BF16),
            pltpu.VMEM((2, 7, half, width), BF16),
            pltpu.VMEM((2, rows, width), F32),
            pltpu.VMEM((rows, width), BF16),
            pltpu.VMEM((rows, width), BF16),
            pltpu.VMEM((rows, width), F32),
            pltpu.VMEM((rows, 128), F32),
            pltpu.VMEM((RING, 1, rows), F32),
            pltpu.VMEM((2, 7, 1, rows), F32),
            pltpu.VMEM((2, 7, 1, rows), F32),
            dma((4,)),
            dma((1,)),
            dma((2, 7, 2)),
            dma((1,)),
            dma((2, 7, 2)),
            dma((1,)),
            dma((2, 7)),
            dma((3,)),
            dma((3,)),
            dma((2,)),
            dma((2,)),
            dma((1,)),
            dma((1,)),
        ],
        compiler_params=pltpu.CompilerParams(
            collective_id=0, has_side_effects=True, vmem_limit_bytes=48 * 2**20
        ),
        cost_estimate=pl.CostEstimate(
            flops=3 * 2 * 1024 * 512 * width, bytes_accessed=6 * rows * width, transcendentals=0
        ),
    )(image_embed, text_embed, both)
    return pl.pallas_call(
        write_out,
        out_shape=(
            jax.ShapeDtypeStruct((rows,), F32),
            jax.ShapeDtypeStruct((rows, width), F32),
            jax.ShapeDtypeStruct((rows, width), F32),
        ),
        in_specs=[vmem] * 7,
        out_specs=(anywhere, anywhere, anywhere),
        scratch_shapes=[pltpu.VMEM((rows,), F32), pltpu.VMEM((2, rows // 4, width), F32), dma((6,))],
        compiler_params=pltpu.CompilerParams(vmem_limit_bytes=4 * 2**20),
        cost_estimate=pl.CostEstimate(flops=0, bytes_accessed=16 * rows * width, transcendentals=0),
    )(*results, both)


def solution(mesh):
    placed = (P(("group", "blk"), None), P(("group", "blk"), None), P(), P())
    return jax.shard_map(
        per_device,
        mesh=mesh,
        in_specs=placed,
        out_specs=(P(("group", "blk")), P(("group", "blk"), None), P(("group", "blk"), None)),
        check_vma=False,
    )
```
